32 devices in a mesh: dp: 4 (over y, x), fsdp: 8 (over z, core).
Axes of the slice: x: 2, y: 2, z: 4, core: 2. Of those that a mesh axis runs over, the one named last changes fastest.
Arguments:
- inputs: bfloat16 [65536, 1280], P(('dp', 'fsdp')), may hold values from -6 to 6
- lengths: int32 [32, 8], P(('dp', 'fsdp')), may hold values from 1 to 1024, 2048 in all within a row
- keep_mask: int32 [65536], P(('dp', 'fsdp')), may hold values 0 or 1
- cotangent: bfloat16 [65536, 1280], P(('dp', 'fsdp')), may hold values from -6 to 6
- ln1_gain: bfloat16 [1280], P(('dp', 'fsdp')), may hold values from 0.099609375 to 1.8984375
- ln1_bias: bfloat16 [1280], P(('dp', 'fsdp')), may hold values from -3 to 3
- up_weight: bfloat16 [1280, 640], P(('dp', 'fsdp')), may hold values from -0.15625 to 0.15625
- up_bias: bfloat16 [640], P(('dp', 'fsdp')), may hold values from -3 to 3
- ln2_gain: bfloat16 [640], P(('dp', 'fsdp')), may hold values from 0.099609375 to 1.8984375
- ln2_bias: bfloat16 [640], P(('dp', 'fsdp')), may hold values from -3 to 3
- conv_weight: bfloat16 [5, 640, 640], P(None, ('dp', 'fsdp')), may hold values from -0.109375 to 0.109375
- conv_bias: bfloat16 [640], P(('dp', 'fsdp')), may hold values from -3 to 3
- ln3_gain: bfloat16 [640], P(('dp', 'fsdp')), may hold values from 0.099609375 to 1.8984375
- ln3_bias: bfloat16 [640], P(('dp', 'fsdp')), may hold values from -3 to 3
- down_weight: bfloat16 [640, 1280], P(None, ('dp', 'fsdp')), may hold values from -0.3125 to 0.3125
- down_bias: bfloat16 [1280], P(('dp', 'fsdp')), may hold values from -3 to 3
Outputs:
- output: bfloat16 [65536, 1280], P(('dp', 'fsdp'))
- input_grad: float32 [65536, 1280], P(('dp', 'fsdp'))
- up_weight_grad: float32 [1280, 640], P(('dp', 'fsdp'))
- conv_weight_grad: float32 [5, 640, 640], P(None, ('dp', 'fsdp'))
- down_weight_grad: float32 [640, 1280], P(None, ('dp', 'fsdp'))
- ln1_gain_grad: float32 [1280], P(('dp', 'fsdp'))
- ln1_bias_grad: float32 [1280], P(('dp', 'fsdp'))
- up_bias_grad: float32 [640], P(('dp', 'fsdp'))
- ln2_gain_grad: float32 [640], P(('dp', 'fsdp'))
- ln2_bias_grad: float32 [640], P(('dp', 'fsdp'))
- conv_bias_grad: float32 [640], P(('dp', 'fsdp'))
- ln3_gain_grad: float32 [640], P(('dp', 'fsdp'))
- ln3_bias_grad: float32 [640], P(('dp', 'fsdp'))
- down_bias_grad: float32 [1280], P(('dp', 'fsdp'))
The draws below stay inside these ranges and needn't reach their ends.
Inputs may be any that keep to these rules, and one draw needn't show every extreme that they name: `lengths`: each row sums to 2048; the largest entry of every row is 1024.
All inputs are finite; a program needn't handle non-finite values. No bound on the sum of `keep_mask` on one device may be relied on, other than what follows from the above.
Results may differ from the reference program's by a relative error of at most 0.0068.
Values may be sent and summed in bfloat16 or wider, within the bound.
No kernel may reach another device: no remote copies, remote signals or barrier semaphores. Data moves between devices by JAX's collectives and lax.ppermute only.
A program may use at most 192 MiB of HBM per device.

```python
import math
import jax
import jax.numpy as jnp
import numpy as np
from jax import lax

D = 1280
INNER = 640
KERNEL = 5
DILATION = 8
MAXLEN = 1024
TOK_DEV = 2048
SEQ_SLOTS = 8
GROUPS = 32
TOKENS = 65536


def set_ends(values, own_key, least, top_value):
    longest = values.shape.index(max(values.shape))
    spots = []
    for shift in (0, 1):
        where = [jax.random.randint(jax.random.fold_in(own_key, axis), (), 0, length) for axis, length in enumerate(values.shape)]
        where[longest] = (where[longest] + shift) % values.shape[longest]
        spots.append(tuple(where))
    return values.at[spots[0]].set(least).at[spots[1]].set(top_value)


def raised(drawn, key, source, target, parts, factor):
    owner, partner = [(jnp.arange(drawn.shape[dim]) // (drawn.shape[dim] // parts)).reshape([-1 if axis == dim else 1 for axis in range(drawn.ndim)]) for dim in (source, target)]
    chosen = jax.random.permutation(key, parts)[partner]
    strong = (owner == chosen) | (owner == (partner + parts // 2) % parts)
    return jnp.where(strong, factor * drawn, drawn)


def level_of(rng, shape, split, smallest, largest):
    def one(dim, shards_of):
        heights = jax.random.uniform(jax.random.fold_in(jax.random.fold_in(rng, 6), dim), (shards_of,), jnp.float32, smallest / len(split), largest / len(split))
        return jnp.repeat(jnp.exp(heights), shape[dim] // shards_of).reshape((-1,) + (1,) * (len(shape) - dim - 1))

    loudness = one(*split[0])
    for cut in split[1:]:
        loudness = loudness * one(*cut)
    return loudness


def profile(number_of, total, most, skew):
    loads = [(1 << 20) // math.isqrt(standing ** skew) + 1 for standing in range(2, number_of + 1)]
    surplus, counts = total - most - (number_of - 1), [1] * (number_of - 1)
    while surplus > 0:
        free = [i for i in range(number_of - 1) if counts[i] < most]
        mass, budget = sum([loads[i] for i in free]), surplus
        for i in free:
            more = min(most - counts[i], max(1, budget * loads[i] // mass), surplus)
            counts[i] = counts[i] + more
            surplus = surplus - more
    return np.array([most] + counts)


def uneven(rng, amount, total, most, slope):
    if amount == 2:
        one = jax.random.randint(rng, (), max(1, total - most), min(most, total - 1) + 1)
        return jnp.stack([one, total - one])
    tallies = jnp.asarray(profile(amount, total, most, slope), jnp.int32)
    twos = (amount - 1) // 2
    giver, sink = tallies[1:1 + 2 * twos:2], tallies[2:2 + 2 * twos:2]
    slack = jnp.minimum(giver - 1, most - sink)
    shifted = jax.random.randint(jax.random.fold_in(rng, 1), (twos,), 0, 1 << 20) % (slack + 1)
    tallies = tallies.at[1:1 + 2 * twos:2].set(giver - shifted).at[2:2 + 2 * twos:2].set(sink + shifted)
    return tallies[jax.random.permutation(jax.random.fold_in(rng, 2), amount)]


def scatter_about(own_key, dims, scale, most, cuts=(), kind=jnp.bfloat16):
    level = level_of(own_key, dims, cuts, -0.22, 0.18) if cuts else 1.0
    array = jax.random.normal(own_key, dims, jnp.float32) * scale * level
    return jnp.minimum(jnp.maximum(array, -most), most).astype(kind)


def bell_draw_with(rng, extent, scale, most, split, heavy, held_as=jnp.bfloat16):
    array = scale * jax.random.normal(rng, extent, jnp.float32)
    if split:
        array = array * level_of(rng, extent, split, -0.22, 0.18)
    return jnp.clip(raised(array, jax.random.fold_in(rng, 3), *heavy), -most, most).astype(held_as)


def setup_inputs(seed: int = 0) -> dict:
    seeds = jax.random.split(jax.random.key(seed), 17)
    return {
        "inputs": scatter_about(seeds[0], (TOKENS, D), 1.0, 6.0, ((0, 32),)),
        "lengths": jax.vmap(lambda own: uneven(own, SEQ_SLOTS, TOK_DEV, MAXLEN, 2))(jax.random.split(seeds[1], GROUPS)).reshape((GROUPS, SEQ_SLOTS)).astype(jnp.int32),
        "keep_mask": set_ends((jax.random.randint(seeds[2], (TOKENS,), 0, 8) < 7).astype(jnp.int32), jax.random.fold_in(seeds[2], 1), 0, 1),
        "cotangent": bell_draw_with(seeds[3], (TOKENS, D), 1.0, 6.0, ((0, 32),), (0, 1, 32, 2.75)),
        "ln1_gain": jnp.clip(1.0 + 0.18 * jax.random.normal(seeds[4], (D,), jnp.float32), 0.099609375, 1.8984375).astype(jnp.bfloat16),
        "ln1_bias": scatter_about(seeds[5], (D,), 0.5, 3.0, ((0, 32),)),
        "up_weight": scatter_about(seeds[6], (D, INNER), D ** -0.5, 0.15625, ((0, 32),)),
        "up_bias": scatter_about(seeds[7], (INNER,), 0.5, 3.0, ((0, 32),)),
        "ln2_gain": jnp.clip(1.0 + 0.18 * jax.random.normal(seeds[8], (INNER,), jnp.float32), 0.099609375, 1.8984375).astype(jnp.bfloat16),
        "ln2_bias": scatter_about(seeds[9], (INNER,), 0.5, 3.0, ((0, 32),)),
        "conv_weight": scatter_about(seeds[10], (KERNEL, INNER, INNER), (KERNEL * INNER) ** -0.5, 0.109375, ((1, 32),)),
        "conv_bias": scatter_about(seeds[11], (INNER,), 0.5, 3.0, ((0, 32),)),
        "ln3_gain": jnp.clip(1.0 + 0.18 * jax.random.normal(seeds[12], (INNER,), jnp.float32), 0.099609375, 1.8984375).astype(jnp.bfloat16),
        "ln3_bias": scatter_about(seeds[13], (INNER,), 0.5, 3.0, ((0, 32),)),
        "down_weight": scatter_about(seeds[14], (INNER, D), (INNER // 2) ** -0.5, 0.3125, ((1, 32),)),
        "down_bias": scatter_about(seeds[15], (D,), 0.5, 3.0, ((0, 32),)),
    }


@jax.custom_vjp
def low(v):
    return lax.optimization_barrier(v.astype(jnp.bfloat16)).astype(jnp.float32)

@jax.custom_vjp
def low_back(v):
    return v

def low_keep(v):
    return (low(v), None)

def low_pass(kept, grad):
    return (grad,)

def back_keep(v):
    return (v, None)

def back_low(kept, grad):
    return (low(grad),)
low.defvjp(low_keep, low_pass)
low_back.defvjp(back_keep, back_low)

def norm_act(field, gain, shift):
    center = field - lax.optimization_barrier(jnp.mean(field, axis=-1, keepdims=True))
    spread = lax.optimization_barrier(jnp.mean(center * center, axis=-1, keepdims=True))
    return jax.nn.gelu(center * lax.rsqrt(spread + 1e-05) * gain + shift)

def tap_masks(lengths_row, count):
    seq_ends = jnp.cumsum(lengths_row).astype(jnp.int32)
    position = jnp.arange(count, dtype=jnp.int32)
    segment = lax.optimization_barrier(jnp.sum((position[:, None] >= seq_ends[None, :]).astype(jnp.int32), axis=1)).astype(jnp.int32)
    masks = []
    for tap in range(KERNEL):
        source = position + (tap - KERNEL // 2) * DILATION
        inside = (source >= 0) & (source < count)
        matched = segment[jnp.clip(source, 0, count - 1)] == segment
        masks.append(jnp.where(inside & matched, 1.0, 0.0))
    return jnp.stack(masks).astype(jnp.float32)

def shifted_taps(field, masks):
    reach = KERNEL // 2 * DILATION
    count = field.shape[0]
    padded = jnp.pad(field, ((reach, reach), (0, 0)))
    return [padded[tap * DILATION:tap * DILATION + count] * masks[tap][:, None] for tap in range(KERNEL)]

def forward(x_float, params, masks, keep_col):
    up_mat, conv_mat, down_mat, gain_one, bias_one, up_shift, gain_two, bias_two, conv_shift, gain_three, bias_three, down_shift = params
    high = lax.Precision.HIGHEST
    act_one = low(norm_act(x_float, gain_one, bias_one))
    up_out = low_back(jnp.dot(act_one, up_mat, precision=high)) + up_shift
    middle = low(norm_act(up_out, gain_two, bias_two) * keep_col)
    taps = shifted_taps(middle, masks)
    conv_sum = jnp.dot(taps[0], conv_mat[0], precision=high)
    for tap in range(1, KERNEL):
        conv_sum = conv_sum + jnp.dot(taps[tap], conv_mat[tap], precision=high)
    conv_out = low_back(conv_sum) + conv_shift
    act_top = low(norm_act(conv_out, gain_three, bias_three))
    return x_float + low_back(jnp.dot(act_top, down_mat, precision=high)) + down_shift

def reference(inputs, lengths, keep_mask, cotangent, ln1_gain, ln1_bias, up_weight, up_bias, ln2_gain, ln2_bias, conv_weight, conv_bias, ln3_gain, ln3_bias, down_weight, down_bias):
    params = tuple((item.astype(jnp.float32) for item in (up_weight, conv_weight, down_weight, ln1_gain, ln1_bias, up_bias, ln2_gain, ln2_bias, conv_bias, ln3_gain, ln3_bias, down_bias)))
    blocks = (inputs.reshape(GROUPS, TOK_DEV, D), lengths, keep_mask.reshape(GROUPS, TOK_DEV), cotangent.reshape(GROUPS, TOK_DEV, D))

    def one_block(totals, items):
        block_in, block_len, block_keep, block_cot = items
        masks = tap_masks(block_len, TOK_DEV)
        keep_col = block_keep.astype(jnp.float32)[:, None]

        def run(x_float, weights):
            return forward(x_float, weights, masks, keep_col)
        result, back = jax.vjp(run, block_in.astype(jnp.float32), params)
        x_grad, weight_grads = back(block_cot.astype(jnp.float32))
        totals = jax.tree.map(jnp.add, totals, weight_grads)
        return (totals, (result.astype(jnp.bfloat16), x_grad))
    zeros = jax.tree.map(jnp.zeros_like, params)
    totals, outcome = lax.scan(one_block, zeros, blocks)
    outputs, x_grads = outcome
    return (outputs.reshape(TOKENS, D), x_grads.reshape(TOKENS, D), totals[0], totals[1], totals[2], totals[3], totals[4], totals[5], totals[6], totals[7], totals[8], totals[9], totals[10], totals[11])
```

```python
import functools

import jax
import jax.numpy as jnp
from jax import lax
from jax.sharding import Mesh
from jax.sharding import PartitionSpec as P

KERNEL = 5
DILATION = 8
ALL = ("dp", "chip", "core")


def norm_act(field, gain, shift):
    center = field - jnp.mean(field, axis=-1, keepdims=True)
    spread = jnp.mean(center * center, axis=-1, keepdims=True)
    return jax.nn.gelu(center * lax.rsqrt(spread + 1e-05) * gain + shift)


def segments(ends, position):
    return jnp.sum((position[:, None] >= ends[None, :]).astype(jnp.int32), axis=1)


def tap_masks(lengths_row, count):
    ends = jnp.cumsum(lengths_row)
    position = jnp.arange(count, dtype=jnp.int32)
    own = segments(ends, position)
    masks = []
    for tap in range(KERNEL):
        source = position + (tap - KERNEL // 2) * DILATION
        inside = (source >= 0) & (source < count)
        masks.append(jnp.where(inside & (segments(ends, source) == own), 1.0, 0.0))
    return jnp.stack(masks).astype(jnp.float32)


def xor_order(items, me):
    bit = 1
    while bit < len(items):
        there = (me & bit) != 0
        items = [jnp.where(there, items[k ^ bit], items[k]) for k in range(len(items))]
        bit *= 2
    return items


def first_dims(left, right):
    return lax.dot_general(
        left, right, (((0,), (0,)), ((), ())), preferred_element_type=jnp.float32
    )


def last_dims(left, right):
    return lax.dot_general(
        left, right, (((1,), (1,)), ((), ())), preferred_element_type=jnp.float32
    )


def swap(array, axis, size, mask):
    return lax.ppermute(array, axis, [(k, k ^ mask) for k in range(size)])


def gather_axis(array, axis, size, place):
    held = [array] + [swap(array, axis, size, mask) for mask in range(1, size)]
    return jnp.stack(xor_order(held, lax.axis_index(axis)), place)


def scatter_axis(array, axis, size, place):
    blocks = [lax.index_in_dim(array, k, place, False) for k in range(size)]
    blocks = xor_order(blocks, lax.axis_index(axis))
    total = blocks[0]
    for mask in range(1, size):
        arrived = swap(blocks[mask].astype(jnp.bfloat16), axis, size, mask)
        total = total + arrived.astype(jnp.float32)
    return total


def gather_all(block, axes):
    out = gather_axis(block, axes[1][0], axes[1][1], 0)
    out = gather_axis(out, axes[0][0], axes[0][1], 0)
    out = gather_axis(out, axes[2][0], axes[2][1], 2)
    return out.reshape((-1,) + block.shape)


def scatter_all(blocks, axes):
    sizes = tuple(size for _, size in axes)
    out = blocks.reshape(sizes + blocks.shape[1:])
    out = scatter_axis(out, axes[2][0], axes[2][1], 2)
    out = scatter_axis(out, axes[0][0], axes[0][1], 0)
    return scatter_axis(out, axes[1][0], axes[1][1], 0)


def body(
    axes,
    inputs,
    lengths,
    keep_mask,
    cotangent,
    ln1_gain,
    ln1_bias,
    up_weight,
    up_bias,
    ln2_gain,
    ln2_bias,
    conv_weight,
    conv_bias,
    ln3_gain,
    ln3_bias,
    down_weight,
    down_bias,
):
    vectors = (ln1_gain, ln1_bias, up_bias, ln2_gain, ln2_bias, conv_bias, ln3_gain, ln3_bias, down_bias)
    widths = [item.shape[0] for item in vectors]
    devices = axes[0][1] * axes[1][1] * axes[2][1]
    taps_in, inner = conv_weight.shape[1], conv_weight.shape[2]
    small = gather_all(jnp.concatenate(vectors)[None, :], axes)[:, 0]
    full_vectors, at = [], 0
    for width in widths:
        full_vectors.append(small[:, at : at + width].reshape(-1).astype(jnp.float32))
        at += width
    (
        gain_one,
        bias_one,
        up_shift,
        gain_two,
        bias_two,
        conv_shift,
        gain_three,
        bias_three,
        down_shift,
    ) = full_vectors
    up_full = gather_all(up_weight, axes).reshape(-1, inner)
    down_full = gather_all(down_weight.T, axes).reshape(-1, inner)
    conv_all = gather_all(conv_weight.reshape(-1, inner), axes)
    conv_full = conv_all.reshape(devices, KERNEL, taps_in, inner).transpose(1, 0, 2, 3).reshape(KERNEL, -1, inner)
    count = inputs.shape[0]
    reach = KERNEL // 2 * DILATION
    masks = tap_masks(lengths[0], count)
    keep_col = keep_mask.astype(jnp.float32)[:, None]
    x_float = inputs.astype(jnp.float32)
    act_first, back_one = jax.vjp(norm_act, x_float, gain_one, bias_one)
    act_one = act_first.astype(jnp.bfloat16)
    up_out = jnp.dot(act_one, up_full, preferred_element_type=jnp.float32) + up_shift

    def masked_act(field, gain, shift):
        return norm_act(field, gain, shift) * keep_col

    act_second, back_two = jax.vjp(masked_act, up_out, gain_two, bias_two)
    middle = act_second.astype(jnp.bfloat16)
    padded = jnp.pad(middle, ((reach, reach), (0, 0)))
    taps = [
        padded[tap * DILATION : tap * DILATION + count] * masks[tap][:, None].astype(jnp.bfloat16)
        for tap in range(KERNEL)
    ]
    conv_sum = jnp.dot(taps[0], conv_full[0], preferred_element_type=jnp.float32)
    for tap in range(1, KERNEL):
        conv_sum = conv_sum + jnp.dot(taps[tap], conv_full[tap], preferred_element_type=jnp.float32)
    conv_out = conv_sum + conv_shift
    act_third, back_three = jax.vjp(norm_act, conv_out, gain_three, bias_three)
    act_top = act_third.astype(jnp.bfloat16)
    output = (
        x_float + last_dims(act_top, down_full) + down_shift
    ).astype(jnp.bfloat16)
    grad_out = cotangent.astype(jnp.float32)
    down_shift_grad = jnp.sum(grad_out, axis=0)
    down_grad = first_dims(cotangent, act_top)
    top_grad = jnp.dot(cotangent, down_full, preferred_element_type=jnp.float32)
    conv_grad, gain_three_grad, bias_three_grad = back_three(top_grad)
    conv_shift_grad = jnp.sum(conv_grad, axis=0)
    conv_low = conv_grad.astype(jnp.bfloat16)
    conv_grad_weight = jnp.stack([first_dims(tap_in, conv_low) for tap_in in taps])
    padded_grad = jnp.zeros((count + 2 * reach, conv_low.shape[1]), jnp.float32)
    for tap in range(KERNEL):
        term = last_dims(conv_low, conv_full[tap]) * masks[tap][:, None]
        padded_grad = padded_grad.at[tap * DILATION : tap * DILATION + count].add(term)
    middle_grad = padded_grad[reach : reach + count]
    up_grad, gain_two_grad, bias_two_grad = back_two(middle_grad)
    up_shift_grad = jnp.sum(up_grad, axis=0)
    up_low = up_grad.astype(jnp.bfloat16)
    up_grad_weight = first_dims(act_one, up_low)
    act_grad = last_dims(up_low, up_full)
    skip_grad, gain_one_grad, bias_one_grad = back_one(act_grad)
    input_grad = grad_out + skip_grad
    up_own = scatter_all(up_grad_weight.reshape(devices, -1, inner), axes)
    conv_own = scatter_all(
        conv_grad_weight.reshape(KERNEL, devices, taps_in, inner).transpose(1, 0, 2, 3).reshape(devices, -1, inner), axes
    ).reshape(conv_weight.shape)
    down_own = scatter_all(down_grad.reshape(devices, -1, inner), axes).T
    sums = (
        gain_one_grad,
        bias_one_grad,
        up_shift_grad,
        gain_two_grad,
        bias_two_grad,
        conv_shift_grad,
        gain_three_grad,
        bias_three_grad,
        down_shift_grad,
    )
    small_own = scatter_all(
        jnp.concatenate([item.reshape(devices, -1) for item in sums], axis=1)[:, None, :], axes
    )[0]
    owned, at = [up_own, conv_own, down_own], 0
    for width in widths:
        owned.append(small_own[at : at + width])
        at += width
    return (output, input_grad) + tuple(owned)


def solution(mesh):
    rows, columns = mesh.shape["dp"], mesh.shape["fsdp"] // 2
    split = Mesh(mesh.devices.reshape(rows, columns, 2), ALL)
    axes = (("dp", rows), ("chip", columns), ("core", 2))
    in_specs = (
        P(ALL, None),
        P(ALL, None),
        P(ALL),
        P(ALL, None),
        P(ALL),
        P(ALL),
        P(ALL, None),
        P(ALL),
        P(ALL),
        P(ALL),
        P(None, ALL, None),
        P(ALL),
        P(ALL),
        P(ALL),
        P(None, ALL),
        P(ALL),
    )
    out_specs = (
        P(ALL, None),
        P(ALL, None),
        P(ALL, None),
        P(None, ALL, None),
        P(None, ALL),
        P(ALL),
        P(ALL),
        P(ALL),
        P(ALL),
        P(ALL),
        P(ALL),
        P(ALL),
        P(ALL),
        P(ALL),
    )
    return jax.shard_map(functools.partial(body, axes), mesh=split, in_specs=in_specs, out_specs=out_specs, check_vma=False)
```

```python
import functools

import jax
import jax.numpy as jnp
from jax import lax
from jax.experimental import pallas as pl
from jax.experimental.pallas import tpu as pltpu
from jax.sharding import Mesh
from jax.sharding import PartitionSpec as P

KERNEL = 5
DILATION = 8
REACH = KERNEL // 2 * DILATION
ALL = ("dp", "chip", "core")
F32 = jnp.float32
BF16 = jnp.bfloat16
TANH_ONE = 0.7978845608028654
TANH_THREE = TANH_ONE * 0.044715
ROWS = 16
VMEM_BYTES = 56 * 2**20


def xor_order(items, me):
    bit = 1
    while bit < len(items):
        there = (me & bit) != 0
        items = [jnp.where(there, items[k ^ bit], items[k]) for k in range(len(items))]
        bit *= 2
    return items


def swap(array, axis, size, mask):
    return lax.ppermute(array, axis, [(k, k ^ mask) for k in range(size)])


def gather_axis(array, axis, size, place):
    held = [array] + [swap(array, axis, size, mask) for mask in range(1, size)]
    return jnp.stack(xor_order(held, lax.axis_index(axis)), place)


def gather_all(block, axes, order=(1, 0, 2)):
    out, held = block, []
    for axis in order:
        held = sorted(held + [axis])
        out = gather_axis(out, axes[axis][0], axes[axis][1], held.index(axis))
    return out.reshape((-1,) + block.shape)


def scatter_axis(total, axis, size):
    arrived = [swap(total[mask].astype(BF16), axis, size, mask) for mask in range(1, size)]
    kept = total[0].astype(F32)
    for item in arrived:
        kept = kept + item.astype(F32)
    return kept


def scatter_all(kept, sent, axes, order=(0, 1)):
    total = kept.astype(F32) + swap(sent, axes[2][0], axes[2][1], 1).astype(F32)
    if order == (1, 0):
        total = jnp.swapaxes(total, 0, 1)
    for axis in order:
        total = scatter_axis(total, axes[axis][0], axes[axis][1])
    return total


def scatter_exact(kept, sent, axes):
    total = kept + swap(sent, axes[2][0], axes[2][1], 1)
    for axis in (0, 1):
        name, size = axes[axis]
        total = total[0] + sum(swap(total[mask], name, size, mask) for mask in range(1, size))
    return total


def norm(z, width):
    center = z - jnp.sum(z, axis=1, keepdims=True) * (1.0 / width)
    scale = lax.rsqrt(jnp.sum(center * center, axis=1, keepdims=True) * (1.0 / width) + 1e-05)
    return center * scale, scale


def gelu(s):
    square = s * s
    half = 0.5 * s
    return half + half * jnp.tanh(s * (TANH_ONE + TANH_THREE * square))


def gelu_slope(s):
    square = s * s
    t = jnp.tanh(s * (TANH_ONE + TANH_THREE * square))
    return (0.5 + 0.5 * t) + (0.5 * s) * (1.0 - t * t) * (TANH_ONE + 3.0 * TANH_THREE * square)


def norm_back(hat, scale, gain, slope, grad, width):
    by_sum = slope * grad
    by_gain = by_sum * hat
    by_hat = by_sum * gain
    first = jnp.sum(by_hat, axis=1, keepdims=True) * (1.0 / width)
    second = jnp.sum(by_hat * hat, axis=1, keepdims=True) * (1.0 / width)
    return scale * (by_hat - first - hat * second), by_gain, by_sum


def fold(value):
    return value[0:8] + value[8:16]


def chunks(count, body, unroll=4):
    def step(k, carry):
        body(pl.multiple_of(k * ROWS, ROWS))
        return carry

    lax.fori_loop(0, count // ROWS, step, 0, unroll=unroll)


def dot(left, right, left_dim=1, right_dim=0):
    return lax.dot_general(
        left, right, (((left_dim,), (right_dim,)), ((), ())), preferred_element_type=F32
    )


def first_act_kernel(small_ref, x_ref, act_ref, wide_ref, narrow_ref):
    block, width = x_ref.shape

    @pl.when(pl.program_id(0) == 0)
    def _():
        devices = small_ref.shape[0]
        of_wide, of_narrow = width // devices, narrow_ref.shape[1] // devices
        for k in range(devices):
            item = small_ref[k].astype(F32)
            wide_ref[:, k * of_wide : (k + 1) * of_wide] = item[0:8, 0:of_wide]
            narrow_ref[:, k * of_narrow : (k + 1) * of_narrow] = item[8:16, 0:of_narrow]

    gain, bias = wide_ref[0:1, :], wide_ref[1:2, :]

    def body(at):
        hat, _ = norm(x_ref[pl.ds(at, ROWS), :].astype(F32), width)
        act_ref[pl.ds(at, ROWS), :] = gelu(hat * gain + bias).astype(BF16)

    chunks(block, body)


def up_kernel(act_ref, weight_ref, narrow_ref, flags_ref, out_ref, mid_ref):
    block, width = out_ref.shape
    out_ref[...] = dot(act_ref[...], weight_ref[...])
    shift, gain, bias = narrow_ref[0:1, :], narrow_ref[1:2, :], narrow_ref[2:3, :]

    def body(at):
        rows = pl.ds(at, ROWS)
        z = out_ref[rows, :] + shift
        out_ref[rows, :] = z
        hat, _ = norm(z, width)
        mid_ref[rows, :] = (gelu(hat * gain + bias) * flags_ref[rows, 0:1]).astype(BF16)

    chunks(block, body)


def fill_padded(padded_ref, source_ref):
    count, width = source_ref.shape
    padded_ref[0:REACH, :] = jnp.zeros((REACH, width), F32)
    padded_ref[count + REACH : count + 2 * REACH, :] = jnp.zeros((REACH, width), F32)

    def body(at):
        padded_ref[pl.ds(REACH + at, ROWS), :] = source_ref[pl.ds(at, ROWS), :].astype(F32)

    chunks(count, body)


def shifted(padded_ref, flags_ref, start, block, tap):
    at = pl.multiple_of(start + tap * DILATION, DILATION)
    rows = padded_ref[pl.ds(at, block), :]
    if tap != KERNEL // 2:
        rows = rows * flags_ref[:, tap + 1 : tap + 2]
    return rows.astype(BF16)


def conv_kernel(
    mid_ref, pieces_ref, down_ref, cot_ref, narrow_ref, flags_ref, place_ref,
    top_ref, low_ref, weight_ref, sums_ref, wide_sums_ref, kept_ref, sent_ref,
    padded_ref, wide_weight_ref, row_ref, out_ref, grad_ref, down_grad_ref,
):
    step, steps = pl.program_id(0), pl.num_programs(0)
    block, width = out_ref.shape
    devices = pieces_ref.shape[0]
    share = width // devices

    @pl.when(step == 0)
    def _():
        fill_padded(padded_ref, mid_ref)
        for k in range(devices):
            row_ref[...] = pieces_ref[k].astype(F32)
            for tap in range(KERNEL):
                wide_weight_ref[tap, k * share : (k + 1) * share, :] = row_ref[tap * share : (tap + 1) * share, :]
        for tap in range(KERNEL):
            weight_ref[tap] = wide_weight_ref[tap].astype(BF16)
        sums_ref[...] = jnp.zeros_like(sums_ref)
        wide_sums_ref[...] = jnp.zeros_like(wide_sums_ref)
        down_grad_ref[...] = jnp.zeros_like(down_grad_ref)

    start = step * block
    for tap in range(KERNEL):
        term = dot(shifted(padded_ref, flags_ref, start, block, tap), weight_ref[tap])
        out_ref[...] = term if tap == 0 else out_ref[...] + term
    grad_ref[...] = dot(cot_ref[...], down_ref[...])
    shift, gain, bias = narrow_ref[3:4, :], narrow_ref[4:5, :], narrow_ref[5:6, :]

    def body(at):
        rows = pl.ds(at, ROWS)
        hat, scale = norm(out_ref[rows, :] + shift, width)
        s = hat * gain + bias
        square = s * s
        t = jnp.tanh(s * (TANH_ONE + TANH_THREE * square))
        half = 0.5 * s
        top_ref[rows, :] = (half + half * t).astype(BF16)
        slope = (0.5 + 0.5 * t) + half * (1.0 - t * t) * (TANH_ONE + 3.0 * TANH_THREE * square)
        back, by_gain, by_sum = norm_back(hat, scale, gain, slope, grad_ref[rows, :], width)
        low_ref[rows, :] = back.astype(BF16)
        sums_ref[0:8, :] += fold(by_gain)
        sums_ref[8:16, :] += fold(by_sum)
        sums_ref[16:24, :] += fold(back)
        wide_sums_ref[...] += fold(cot_ref[rows, :].astype(F32))

    chunks(block, body)
    down_grad_ref[...] += dot(cot_ref[...], top_ref[...], 0, 0)

    @pl.when(step == steps - 1)
    def _():
        part_out(place_ref, down_grad_ref, kept_ref, sent_ref)


def hand_out(place_ref, device, kept_ref, sent_ref, rows, part):
    m = (device // 2) ^ place_ref[0]

    @pl.when(place_ref[1] == device % 2)
    def _():
        kept_ref[m, rows, 0 : part.shape[1]] = part.astype(kept_ref.dtype)

    @pl.when(place_ref[1] != device % 2)
    def _():
        sent_ref[m, rows, 0 : part.shape[1]] = part.astype(sent_ref.dtype)


def part_out(place_ref, total_ref, kept_ref, sent_ref):
    share = kept_ref.shape[1]
    for device in range(2 * kept_ref.shape[0]):
        part = total_ref[device * share : (device + 1) * share, :]
        hand_out(place_ref, device, kept_ref, sent_ref, slice(None), part)


def conv_weight_kernel(
    low_ref, mid_ref, flags_ref, place_ref, kept_ref, sent_ref, padded_ref, total_ref, row_ref
):
    step, steps = pl.program_id(0), pl.num_programs(0)
    block, width = mid_ref.shape
    chips = kept_ref.shape[0]
    share = width // (2 * chips)

    @pl.when(step == 0)
    def _():
        fill_padded(padded_ref, low_ref)
        total_ref[...] = jnp.zeros_like(total_ref)

    mid = mid_ref[...].T
    for tap in range(KERNEL):
        other = shifted(padded_ref, flags_ref, step * block, block, KERNEL - 1 - tap)
        total_ref[tap] += dot(mid, other)

    @pl.when(step == steps - 1)
    def _():
        for device in range(2 * chips):
            for tap in range(KERNEL):
                row_ref[tap * share : (tap + 1) * share, :] = total_ref[tap, device * share : (device + 1) * share, :]
            hand_out(place_ref, device, kept_ref, sent_ref, slice(None), row_ref[...])


def mid_grad_kernel(
    low_ref, weight_ref, up_out_ref, act_ref, narrow_ref, flags_ref, place_ref,
    up_low_ref, sums_ref, kept_ref, sent_ref,
    padded_ref, grad_ref, total_ref,
):
    step, steps = pl.program_id(0), pl.num_programs(0)
    block, width = up_out_ref.shape

    @pl.when(step == 0)
    def _():
        fill_padded(padded_ref, low_ref)
        sums_ref[...] = jnp.zeros_like(sums_ref)
        total_ref[...] = jnp.zeros_like(total_ref)

    for tap in range(KERNEL):
        other = shifted(padded_ref, flags_ref, step * block, block, KERNEL - 1 - tap)
        term = dot(other, weight_ref[tap], 1, 1)
        grad_ref[...] = term if tap == 0 else grad_ref[...] + term
    gain, bias = narrow_ref[1:2, :], narrow_ref[2:3, :]

    def body(at):
        rows = pl.ds(at, ROWS)
        hat, scale = norm(up_out_ref[rows, :], width)
        slope = gelu_slope(hat * gain + bias) * flags_ref[rows, 0:1]
        back, by_gain, by_sum = norm_back(hat, scale, gain, slope, grad_ref[rows, :], width)
        up_low_ref[rows, :] = back.astype(BF16)
        sums_ref[0:8, :] += fold(by_gain)
        sums_ref[8:16, :] += fold(by_sum)
        sums_ref[16:24, :] += fold(back)

    chunks(block, body)
    total_ref[...] += dot(act_ref[...], up_low_ref[...], 0, 0)

    @pl.when(step == steps - 1)
    def _():
        part_out(place_ref, total_ref, kept_ref, sent_ref)


def input_grad_kernel(
    up_low_ref, weight_ref, x_ref, cot_ref, wide_ref, top_sums_ref, mid_sums_ref, cot_sums_ref, place_ref,
    out_ref, kept_ref, sent_ref,
    grad_ref, sums_ref, wide_row_ref, narrow_row_ref,
):
    step, steps = pl.program_id(0), pl.num_programs(0)
    block, width = out_ref.shape

    @pl.when(step == 0)
    def _():
        sums_ref[...] = jnp.zeros_like(sums_ref)

    grad_ref[...] = dot(up_low_ref[...], weight_ref[...], 1, 1)
    gain, bias = wide_ref[0:1, :], wide_ref[1:2, :]

    def body(at):
        rows = pl.ds(at, ROWS)
        hat, scale = norm(x_ref[rows, :].astype(F32), width)
        back, by_gain, by_sum = norm_back(hat, scale, gain, gelu_slope(hat * gain + bias), grad_ref[rows, :], width)
        out_ref[rows, :] = cot_ref[rows, :].astype(F32) + back
        sums_ref[0:8, :] += fold(by_gain)
        sums_ref[8:16, :] += fold(by_sum)

    chunks(block, body, unroll=2)

    @pl.when(step == steps - 1)
    def _():
        def row(ref, k):
            return jnp.sum(ref[8 * k : 8 * k + 8, :], axis=0, keepdims=True)

        wide_row_ref[...] = jnp.zeros_like(wide_row_ref)
        narrow_row_ref[...] = jnp.zeros_like(narrow_row_ref)
        for at, (ref, k) in enumerate(((sums_ref, 0), (sums_ref, 1), (cot_sums_ref, 0))):
            wide_row_ref[at : at + 1, :] = row(ref, k)
        rows = ((mid_sums_ref, 2), (mid_sums_ref, 0), (mid_sums_ref, 1), (top_sums_ref, 2), (top_sums_ref, 0), (top_sums_ref, 1))
        for at, (ref, k) in enumerate(rows):
            narrow_row_ref[at : at + 1, :] = row(ref, k)
        chips = kept_ref.shape[0]
        wide, narrow = width // (2 * chips), narrow_row_ref.shape[1] // (2 * chips)
        kept_ref[...] = jnp.zeros_like(kept_ref)
        sent_ref[...] = jnp.zeros_like(sent_ref)
        for device in range(2 * chips):
            wide_part = wide_row_ref[:, device * wide : (device + 1) * wide]
            narrow_part = narrow_row_ref[:, device * narrow : (device + 1) * narrow]
            hand_out(place_ref, device, kept_ref, sent_ref, slice(0, 8), wide_part)
            hand_out(place_ref, device, kept_ref, sent_ref, slice(8, 16), narrow_part)


def output_kernel(x_ref, top_ref, weight_ref, wide_ref, out_ref):
    product = dot(top_ref[...], weight_ref[...], 1, 1)
    out_ref[...] = (x_ref[...].astype(F32) + product + wide_ref[2:3, :]).astype(BF16)


def call(kernel, name, grid, ins, outs, scratch, flops, args):
    def spec(shape, rows):
        if rows == "smem":
            return pl.BlockSpec(memory_space=pltpu.SMEM)
        if rows is None:
            return pl.BlockSpec(shape, lambda i: (0,) * len(shape))
        return pl.BlockSpec((rows,) + tuple(shape[1:]), lambda i: (i,) + (0,) * (len(shape) - 1))

    moved = sum(a.size * a.dtype.itemsize for a in args) + sum(
        jax.ShapeDtypeStruct(*o[0]).size * jnp.dtype(o[0][1]).itemsize for o in outs
    )
    return pl.pallas_call(
        kernel,
        name=name,
        grid=(grid,),
        in_specs=[spec(a.shape, rows) for a, rows in zip(args, ins)],
        out_specs=[spec(o[0][0], o[1]) for o in outs],
        out_shape=[jax.ShapeDtypeStruct(*o[0]) for o in outs],
        scratch_shapes=scratch,
        compiler_params=pltpu.CompilerParams(vmem_limit_bytes=VMEM_BYTES),
        cost_estimate=pl.CostEstimate(flops=flops, bytes_accessed=moved, transcendentals=0),
    )(*args)


def flags_of(lengths_row, keep_mask):
    count = keep_mask.shape[0]
    ends = jnp.cumsum(lengths_row)
    position = jnp.arange(count, dtype=jnp.int32)[:, None]

    def segment(at):
        return jnp.sum((at >= ends[None, :]).astype(jnp.int32), axis=1, keepdims=True)

    own = segment(position)
    columns = [keep_mask[:, None] != 0]
    for tap in range(KERNEL):
        source = position + (tap - KERNEL // 2) * DILATION
        columns.append((source >= 0) & (source < count) & (segment(source) == own))
    columns += [columns[0]] * (8 - len(columns))
    return jnp.concatenate([column.astype(F32) for column in columns], axis=1)


def pack_small(wide, narrow):
    out = jnp.zeros((16, 128), BF16)
    for first, group in ((0, wide), (8, narrow)):
        for k, item in enumerate(group):
            out = out + jnp.pad(item[None, :], ((first + k, 15 - first - k), (0, 128 - item.shape[0])))
    return out


def body(
    axes,
    inputs,
    lengths,
    keep_mask,
    cotangent,
    ln1_gain,
    ln1_bias,
    up_weight,
    up_bias,
    ln2_gain,
    ln2_bias,
    conv_weight,
    conv_bias,
    ln3_gain,
    ln3_bias,
    down_weight,
    down_bias,
):
    count, model = inputs.shape
    inner = up_weight.shape[1]
    dp, columns = axes[0][1], axes[1][1]
    chips = dp * columns
    place = jnp.stack(
        [lax.axis_index("dp") * columns + lax.axis_index("chip"), lax.axis_index("core")]
    ).astype(jnp.int32)
    flags = flags_of(lengths[0], keep_mask)

    small = gather_all(
        pack_small(
            (ln1_gain, ln1_bias, down_bias),
            (up_bias, ln2_gain, ln2_bias, conv_bias, ln3_gain, ln3_bias),
        ),
        axes,
    )
    up_full = gather_all(up_weight, axes).reshape(model, inner)
    conv_pieces = gather_all(conv_weight.reshape(-1, inner), axes)
    down_full = gather_all(down_weight.T, axes).reshape(model, inner)

    full = functools.partial
    block = 256
    steps = count // block
    wide_up = 2 * count * model * inner
    wide_conv = 2 * count * KERNEL * inner * inner

    act_one, wide, narrow = call(
        first_act_kernel, "first_act", steps, (None, block),
        [(((count, model), BF16), block), (((8, model), F32), None), (((8, inner), F32), None)],
        [], 20 * count * model, (small, inputs),
    )
    up_out, mid = call(
        up_kernel, "up", steps, (block, None, None, block),
        [(((count, inner), F32), block), (((count, inner), BF16), block)],
        [], wide_up, (act_one, up_full, narrow, flags),
    )
    share, conv_share = model // (2 * chips), KERNEL * inner // (2 * chips)
    top, low, conv_full, top_sums, cot_sums, down_kept, down_sent = call(
        conv_kernel, "conv", steps, (None, None, None, block, None, block, "smem"),
        [
            (((count, inner), BF16), block),
            (((count, inner), BF16), block),
            (((KERNEL, inner, inner), BF16), None),
            (((24, inner), F32), None),
            (((8, model), F32), None),
            (((chips, share, inner), F32), None),
            (((chips, share, inner), BF16), None),
        ],
        [
            pltpu.VMEM((count + 2 * REACH, inner), F32),
            pltpu.VMEM((KERNEL, inner, inner), F32),
            pltpu.VMEM((conv_share, inner), F32),
            pltpu.VMEM((block, inner), F32),
            pltpu.VMEM((block, inner), F32),
            pltpu.VMEM((model, inner), F32),
        ],
        wide_conv + 2 * wide_up, (mid, conv_pieces, down_full, cotangent, narrow, flags, place),
    )
    down_own = scatter_all(
        down_kept.reshape(dp, columns, share, inner), down_sent.reshape(dp, columns, share, inner), axes, (1, 0)
    )
    conv_kept, conv_sent = call(
        conv_weight_kernel, "conv_weight", steps, (None, block, block, "smem"),
        [(((chips, conv_share, inner), F32), None), (((chips, conv_share, inner), BF16), None)],
        [
            pltpu.VMEM((count + 2 * REACH, inner), F32),
            pltpu.VMEM((KERNEL, inner, inner), F32),
            pltpu.VMEM((conv_share, inner), F32),
        ],
        wide_conv, (low, mid, flags, place),
    )
    conv_own = scatter_all(
        conv_kept.reshape(dp, columns, conv_share, inner), conv_sent.reshape(dp, columns, conv_share, inner), axes
    )
    up_low, mid_sums, up_kept, up_sent = call(
        mid_grad_kernel, "mid_grad", steps, (None, None, block, block, None, block, "smem"),
        [
            (((count, inner), BF16), block),
            (((24, inner), F32), None),
            (((chips, share, inner), F32), None),
            (((chips, share, inner), BF16), None),
        ],
        [
            pltpu.VMEM((count + 2 * REACH, inner), F32),
            pltpu.VMEM((block, inner), F32),
            pltpu.VMEM((model, inner), F32),
        ],
        wide_conv + wide_up, (low, conv_full, up_out, act_one, narrow, flags, place),
    )
    up_own = scatter_all(
        up_kept.reshape(dp, columns, share, inner), up_sent.reshape(dp, columns, share, inner), axes
    )
    input_grad, small_kept, small_sent = call(
        input_grad_kernel, "input_grad", steps,
        (block, None, block, block, None, None, None, None, "smem"),
        [
            (((count, model), F32), block),
            (((chips, 16, 128), F32), None),
            (((chips, 16, 128), F32), None),
        ],
        [
            pltpu.VMEM((block, model), F32),
            pltpu.VMEM((16, model), F32),
            pltpu.VMEM((8, model), F32),
            pltpu.VMEM((8, inner), F32),
        ],
        wide_up, (up_low, up_full, inputs, cotangent, wide, top_sums, mid_sums, cot_sums, place),
    )
    small_own = scatter_exact(
        small_kept.reshape(dp, columns, 16, 128), small_sent.reshape(dp, columns, 16, 128), axes
    )
    (output,) = call(
        output_kernel, "output", steps, (block, block, None, None),
        [(((count, model), BF16), block)],
        [], wide_up, (inputs, top, down_full, wide),
    )
    wide_row, narrow_row = up_weight.shape[0], conv_weight.shape[1]
    sums = [small_own[at, :wide_row] for at in range(2)]
    sums += [small_own[8 + at, :narrow_row] for at in range(6)]
    sums.append(small_own[2, :wide_row])
    return (output, input_grad, up_own, conv_own.reshape(conv_weight.shape), down_own.T) + tuple(sums)


def solution(mesh):
    rows, columns = mesh.shape["dp"], mesh.shape["fsdp"] // 2
    split = Mesh(mesh.devices.reshape(rows, columns, 2), ALL)
    axes = (("dp", rows), ("chip", columns), ("core", 2))
    by_row = P(ALL)
    by_second = P(None, ALL)
    in_specs = [by_row] * 16
    in_specs[10] = in_specs[14] = by_second
    out_specs = [by_row] * 14
    out_specs[3] = out_specs[4] = by_second
    return jax.shard_map(
        functools.partial(body, axes),
        mesh=split,
        in_specs=tuple(in_specs),
        out_specs=tuple(out_specs),
        check_vma=False,
    )
```

```python
import functools

import jax
import jax.numpy as jnp
from jax import lax
from jax.experimental import pallas as pl
from jax.experimental.pallas import tpu as pltpu
from jax.sharding import Mesh
from jax.sharding import PartitionSpec as P

KERNEL = 5
DILATION = 8
REACH = KERNEL // 2 * DILATION
ALL = ("dp", "chip", "core")
F32 = jnp.float32
BF16 = jnp.bfloat16
TANH_ONE = 0.7978845608028654
TANH_THREE = TANH_ONE * 0.044715
ROWS = 16
VMEM_BYTES = 56 * 2**20


def swap(array, axis, size, mask):
    return lax.ppermute(array, axis, [(k, k ^ mask) for k in range(size)])


def after(value, *others):
    return lax.optimization_barrier((value, *others))[0]


def gather_stage(block, axis):
    name, size = axis
    return [block] + [swap(block, name, size, mask) for mask in range(1, size)]


def core_stage(pieces, axes):
    return pieces + [swap(piece, axes[2][0], axes[2][1], 1) for piece in pieces]


def scatter_stage(total, axis):
    name, size = axis
    arrived = [swap(total[mask].astype(BF16), name, size, mask) for mask in range(1, size)]
    return total[0], arrived


def add_up(kept, arrived):
    total = kept.astype(F32)
    for item in arrived:
        total = total + item.astype(F32)
    return total


def exact_stage(total, axis):
    name, size = axis
    return total[0] + sum(swap(total[mask], name, size, mask) for mask in range(1, size))


def norm(z, width):
    center = z - jnp.sum(z, axis=1, keepdims=True) * (1.0 / width)
    scale = lax.rsqrt(jnp.sum(center * center, axis=1, keepdims=True) * (1.0 / width) + 1e-05)
    return center * scale, scale


def pipelined(product, rest):
    step, last = pl.program_id(0), pl.num_programs(0) - 1

    @pl.when(step == 0)
    def _():
        product()

    @pl.when((step > 0) & (step < last))
    def _():
        rest()
        product()

    @pl.when(step == last)
    def _():
        rest()


def half_gelu(h):
    q = h * h
    t = jnp.tanh(h * (2.0 * TANH_ONE + 8.0 * TANH_THREE * q))
    return q, t, 1.0 + t


def double_slope(h, q, t, one_t):
    return one_t * (1.0 + (1.0 - t) * (h * (2.0 * TANH_ONE + 24.0 * TANH_THREE * q)))


def back_parts(hat, scale, half_gain, slope2, grad, width):
    by_sum = slope2 * grad
    by_gain = by_sum * hat
    by_hat = by_sum * half_gain
    first = jnp.sum(by_hat, axis=1, keepdims=True) * (scale * (1.0 / width))
    second = jnp.sum(by_hat * hat, axis=1, keepdims=True) * (scale * (1.0 / width))
    return scale * by_hat - first - hat * second, by_gain, by_sum


def fold(value):
    return value[0:8] + value[8:16]


def chunks(count, body, unroll=4):
    def step(k, carry):
        body(pl.multiple_of(k * ROWS, ROWS))
        return carry

    lax.fori_loop(0, count // ROWS, step, 0, unroll=unroll)


def dot(left, right, left_dim=1, right_dim=0):
    return lax.dot_general(
        left, right, (((left_dim,), (right_dim,)), ((), ())), preferred_element_type=F32
    )


def piece_copies(pieces, place_ref, hold_ref, semaphores):
    half = len(pieces) // 2
    columns = pieces[0].shape[0]
    copies = []
    for c in range(2):
        for o in range(half):
            for i in range(columns):
                chip = (place_ref[0] ^ o) * columns + (place_ref[1] ^ i)
                target = hold_ref.at[2 * chip + (place_ref[2] ^ c)]
                copies.append(pltpu.make_async_copy(pieces[c * half + o].at[i], target, semaphores.at[len(copies)]))
    return copies


def first_act_kernel(*refs):
    pieces, rest = refs[: len(refs) - 9], refs[len(refs) - 9 :]
    x_ref, place_ref, act_ref, weight_ref, wide_ref, narrow_ref, hold_ref, wide_weight_ref, semaphores = rest
    block, width = x_ref.shape

    @pl.when(pl.program_id(0) == 0)
    def _():
        parts = [piece.at[o] for piece in pieces for o in range(piece.shape[0])]
        copies = piece_copies(parts, place_ref, hold_ref, semaphores)
        for copy in copies:
            copy.start()
        for copy in copies:
            copy.wait()
        devices = hold_ref.shape[0]
        of_wide, of_narrow = width // devices, narrow_ref.shape[1] // devices
        for k in range(devices):
            item = hold_ref[k].astype(F32)
            small = item[item.shape[0] - 8 :, :]
            wide_ref[:, k * of_wide : (k + 1) * of_wide] = small[:, 0:of_wide]
            narrow_ref[:, k * of_narrow : (k + 1) * of_narrow] = small[:, 128 : 128 + of_narrow]
            wide_weight_ref[k * of_wide : (k + 1) * of_wide, :] = item[0:of_wide, :]
        weight_ref[...] = wide_weight_ref[...].astype(BF16)

    gain, bias = 0.5 * wide_ref[0:1, :], 0.5 * wide_ref[1:2, :]

    def body(at):
        hat, _ = norm(x_ref[pl.ds(at, ROWS), :].astype(F32), width)
        h = hat * gain + bias
        act_ref[pl.ds(at, ROWS), :] = (h * half_gelu(h)[2]).astype(BF16)

    chunks(block, body)


def up_kernel(act_ref, weight_ref, narrow_ref, flags_ref, out_ref, mid_ref, z_ref, next_ref):
    block, width = out_ref.shape

    def product():
        next_ref[...] = dot(act_ref[...], weight_ref[...])
        z_ref[...] = next_ref[...]

    def rest():
        shift, gain, bias = narrow_ref[0:1, :], 0.5 * narrow_ref[1:2, :], 0.5 * narrow_ref[2:3, :]
        for at in range(0, block, ROWS):
            rows = slice(at, at + ROWS)
            z = z_ref[rows, :] + shift
            out_ref[rows, :] = z
            hat, _ = norm(z, width)
            h = hat * gain + bias
            mid_ref[rows, :] = (h * half_gelu(h)[2] * flags_ref[rows, 0:1]).astype(BF16)

    pipelined(product, rest)


def fill_padded(padded_ref, source_ref):
    count, width = source_ref.shape
    padded_ref[0, 0:REACH, :] = jnp.zeros((REACH, width), BF16)
    padded_ref[0, count + REACH : count + 2 * REACH, :] = jnp.zeros((REACH, width), BF16)
    padded_ref[0, REACH : count + REACH, :] = source_ref[...]
    padded_ref[1, 0 : count + REACH, :] = padded_ref[0, DILATION : count + REACH + DILATION, :]


def shifted(padded_ref, flags, start, block, tap):
    which, at = tap % 2, start + tap // 2 * (2 * DILATION)
    if not isinstance(at, int):
        at = pl.multiple_of(at, 2 * DILATION)
    rows = padded_ref[which, pl.ds(at, block), :]
    if tap != KERNEL // 2:
        rows = rows * flags[:, tap + 1 : tap + 2]
    return rows


def conv_kernel(*refs):
    pieces, rest_refs = refs[: len(refs) - 22], refs[len(refs) - 22 :]
    (
        mid_ref, cot_ref, narrow_ref, now_flags_ref, place_ref,
        top_ref, low_ref, flat_ref, down_ref, sums_ref, wide_sums_ref,
        padded_ref, hold_ref, wide_weight_ref, grad_weight_ref, weight_ref, taps_ref,
        out_ref, grad_ref, next_out_ref, next_grad_ref, semaphores,
    ) = rest_refs
    step = pl.program_id(0)
    block, width = out_ref.shape
    model, devices = down_ref.shape[0], hold_ref.shape[0]
    share, conv_share = model // devices, width // devices

    @pl.when(step == 0)
    def _():
        copies = piece_copies(pieces, place_ref, hold_ref, semaphores)
        for copy in copies:
            copy.start()
        fill_padded(padded_ref, mid_ref)
        sums_ref[...] = jnp.zeros_like(sums_ref)
        wide_sums_ref[...] = jnp.zeros_like(wide_sums_ref)
        for copy in copies:
            copy.wait()
        for k in range(devices):
            item = hold_ref[k].astype(F32)
            grad_weight_ref[k * share : (k + 1) * share, :] = item[0:share, :]
            for tap in range(KERNEL):
                rows = slice(tap * width + k * conv_share, tap * width + (k + 1) * conv_share)
                first = share + tap * conv_share
                wide_weight_ref[rows, :] = item[first : first + conv_share, :]
        down_ref[...] = grad_weight_ref[...].astype(BF16)
        for tap in range(KERNEL):
            part = wide_weight_ref[tap * width : (tap + 1) * width, :].astype(BF16)
            weight_ref[tap * width : (tap + 1) * width, :] = part
            flat_ref[:, tap * width : (tap + 1) * width] = part

    def product():
        start = jnp.minimum(step, pl.num_programs(0) - 2) * block
        flags = now_flags_ref[...].astype(BF16)
        for tap in range(KERNEL):
            taps_ref[:, tap * width : (tap + 1) * width] = shifted(padded_ref, flags, start, block, tap)
        next_out_ref[...] = dot(taps_ref[...], weight_ref[...])
        next_grad_ref[...] = dot(cot_ref[...], down_ref[...])
        total = wide_sums_ref[...]
        for at in range(0, block, ROWS):
            total += fold(cot_ref[at : at + ROWS, :].astype(F32))
        wide_sums_ref[...] = total
        out_ref[...] = next_out_ref[...]
        grad_ref[...] = next_grad_ref[...]

    def rest():
        shift, gain, bias = narrow_ref[3:4, :], 0.5 * narrow_ref[4:5, :], 0.5 * narrow_ref[5:6, :]
        totals = [sums_ref[8 * k : 8 * k + 8, :] for k in range(3)]
        for at in range(0, block, ROWS):
            rows = slice(at, at + ROWS)
            hat, scale = norm(out_ref[rows, :] + shift, width)
            h = hat * gain + bias
            q, t, one_t = half_gelu(h)
            top_ref[rows, :] = (h * one_t).astype(BF16)
            slope2 = double_slope(h, q, t, one_t)
            back, by_gain, by_sum = back_parts(hat, scale, gain, slope2, grad_ref[rows, :], width)
            low_ref[rows, :] = back.astype(BF16)
            for k, part in enumerate((by_gain, by_sum, back)):
                totals[k] += fold(part)
        for k in range(3):
            sums_ref[8 * k : 8 * k + 8, :] = totals[k]

    pipelined(product, rest)


def hand_out(place_ref, device, columns, ready_ref, rows, part):
    chip = device // 2
    m, n = (chip // columns) ^ place_ref[0], (chip % columns) ^ place_ref[1]
    which = (device % 2) ^ place_ref[2]
    ready_ref[which, m, n, rows, 0 : part.shape[1]] = part.astype(ready_ref.dtype)


def send_out(ready_ref, kept_hbm, sent_hbm, semaphores):
    copies = [
        pltpu.make_async_copy(ready_ref.at[k], target, semaphores.at[k])
        for k, target in enumerate((kept_hbm, sent_hbm))
    ]
    for copy in copies:
        copy.start()
    for copy in copies:
        copy.wait()


def weights_kernel(
    low_ref, mid_ref, top_hbm, cot_hbm, flags_ref, place_ref, kept_hbm, sent_hbm,
    padded_ref, total_ref, row_ref, top_ref, cot_ref, down_total_ref, ready_ref, semaphores, out_semaphores,
):
    count, width = mid_ref.shape
    columns = ready_ref.shape[2]
    devices = 2 * ready_ref.shape[1] * columns
    share, wide_share = width // devices, cot_ref.shape[1] // devices
    copies = (
        pltpu.make_async_copy(top_hbm, top_ref, semaphores.at[0]),
        pltpu.make_async_copy(cot_hbm, cot_ref, semaphores.at[1]),
    )
    for copy in copies:
        copy.start()
    fill_padded(padded_ref, low_ref)
    flags = flags_ref[...].astype(BF16)
    mid = mid_ref[...].T
    for tap in range(KERNEL):
        total_ref[tap] = dot(mid, shifted(padded_ref, flags, 0, count, KERNEL - 1 - tap))
    for copy in copies:
        copy.wait()
    down_total_ref[...] = dot(cot_ref[...], top_ref[...], 0, 0)
    row_ref[...] = jnp.zeros_like(row_ref)
    for device in range(devices):
        slot = device % row_ref.shape[0]
        row_ref[slot, 0:wide_share, :] = down_total_ref[device * wide_share : (device + 1) * wide_share, :]
        for tap in range(KERNEL):
            part = total_ref[tap, device * share : (device + 1) * share, :]
            row_ref[slot, wide_share + tap * share : wide_share + (tap + 1) * share, :] = part
        hand_out(place_ref, device, columns, ready_ref, slice(None), row_ref[slot])
    send_out(ready_ref, kept_hbm, sent_hbm, out_semaphores)


def up_weight_kernel(act_ref, low_ref, place_ref, kept_hbm, sent_hbm, total_ref, ready_ref, out_semaphores):
    step, steps = pl.program_id(0), pl.num_programs(0)
    total_ref[...] = dot(act_ref[...], low_ref[...], 0, 0)
    share = ready_ref.shape[3]
    devices = total_ref.shape[0] // share
    for k in range(devices):
        part = total_ref[k * share : (k + 1) * share, :]
        hand_out(place_ref, step * devices + k, ready_ref.shape[2], ready_ref, slice(None), part)

    @pl.when(step == steps - 1)
    def _():
        send_out(ready_ref, kept_hbm, sent_hbm, out_semaphores)


def mid_grad_kernel(
    low_ref, flat_ref, up_out_ref, narrow_ref, now_flags_ref, flags_ref,
    up_low_ref, sums_ref,
    padded_ref, taps_ref, grad_ref, next_ref,
):
    step = pl.program_id(0)
    block, width = up_out_ref.shape

    @pl.when(step == 0)
    def _():
        fill_padded(padded_ref, low_ref)
        sums_ref[...] = jnp.zeros_like(sums_ref)

    def product():
        start = jnp.minimum(step, pl.num_programs(0) - 2) * block
        flags = now_flags_ref[...].astype(BF16)
        for tap in range(KERNEL):
            taps_ref[:, tap * width : (tap + 1) * width] = shifted(padded_ref, flags, start, block, KERNEL - 1 - tap)
        next_ref[...] = dot(taps_ref[...], flat_ref[...], 1, 1)
        grad_ref[...] = next_ref[...]

    def rest():
        gain, bias = 0.5 * narrow_ref[1:2, :], 0.5 * narrow_ref[2:3, :]
        totals = [sums_ref[8 * k : 8 * k + 8, :] for k in range(3)]
        for at in range(0, block, ROWS):
            rows = slice(at, at + ROWS)
            hat, scale = norm(up_out_ref[rows, :], width)
            h = hat * gain + bias
            slope2 = double_slope(h, *half_gelu(h))
            grad = grad_ref[rows, :] * flags_ref[rows, 0:1]
            back, by_gain, by_sum = back_parts(hat, scale, gain, slope2, grad, width)
            up_low_ref[rows, :] = back.astype(BF16)
            for k, part in enumerate((by_gain, by_sum, back)):
                totals[k] += fold(part)
        for k in range(3):
            sums_ref[8 * k : 8 * k + 8, :] = totals[k]

    pipelined(product, rest)


def input_grad_kernel(
    up_low_ref, weight_ref, x_ref, cot_ref, wide_ref, top_sums_ref, mid_sums_ref, cot_sums_ref, place_ref,
    out_ref, kept_hbm, sent_hbm,
    grad_ref, next_ref, sums_ref, wide_row_ref, narrow_row_ref, ready_ref, out_semaphores,
):
    step, steps = pl.program_id(0), pl.num_programs(0)
    block, width = out_ref.shape

    @pl.when(step == 0)
    def _():
        sums_ref[...] = jnp.zeros_like(sums_ref)

    def product():
        next_ref[...] = dot(up_low_ref[...], weight_ref[...], 1, 1)
        grad_ref[...] = next_ref[...]

    def rest():
        gain, bias = 0.5 * wide_ref[0:1, :], 0.5 * wide_ref[1:2, :]
        by_gains, by_sums = sums_ref[0:8, :], sums_ref[8:16, :]
        for at in range(0, block, ROWS):
            rows = slice(at, at + ROWS)
            hat, scale = norm(x_ref[rows, :].astype(F32), width)
            h = hat * gain + bias
            slope2 = double_slope(h, *half_gelu(h))
            back, by_gain, by_sum = back_parts(hat, scale, gain, slope2, grad_ref[rows, :], width)
            out_ref[rows, :] = cot_ref[rows, :].astype(F32) + back
            by_gains += fold(by_gain)
            by_sums += fold(by_sum)
        sums_ref[0:8, :] = by_gains
        sums_ref[8:16, :] = by_sums

    pipelined(product, rest)

    @pl.when(step == steps - 1)
    def _():
        def row(ref, k):
            return jnp.sum(ref[8 * k : 8 * k + 8, :], axis=0, keepdims=True)

        wide_row_ref[...] = jnp.zeros_like(wide_row_ref)
        narrow_row_ref[...] = jnp.zeros_like(narrow_row_ref)
        for at, (ref, k, factor) in enumerate(((sums_ref, 0, 0.5), (sums_ref, 1, 0.5), (cot_sums_ref, 0, 1.0))):
            wide_row_ref[at : at + 1, :] = factor * row(ref, k)
        rows = (
            (mid_sums_ref, 2, 1.0),
            (mid_sums_ref, 0, 0.5),
            (mid_sums_ref, 1, 0.5),
            (top_sums_ref, 2, 1.0),
            (top_sums_ref, 0, 0.5),
            (top_sums_ref, 1, 0.5),
        )
        for at, (ref, k, factor) in enumerate(rows):
            narrow_row_ref[at : at + 1, :] = factor * row(ref, k)
        columns = ready_ref.shape[2]
        devices = 2 * ready_ref.shape[1] * columns
        wide, narrow = width // devices, narrow_row_ref.shape[1] // devices
        ready_ref[...] = jnp.zeros_like(ready_ref)
        for device in range(devices):
            wide_part = wide_row_ref[:, device * wide : (device + 1) * wide]
            narrow_part = narrow_row_ref[:, device * narrow : (device + 1) * narrow]
            hand_out(place_ref, device, columns, ready_ref, slice(0, 8), wide_part)
            hand_out(place_ref, device, columns, ready_ref, slice(8, 16), narrow_part)
        send_out(ready_ref, kept_hbm, sent_hbm, out_semaphores)


def output_kernel(x_ref, top_ref, weight_ref, wide_ref, out_ref):
    product = dot(top_ref[...], weight_ref[...], 1, 1)
    out_ref[...] = (x_ref[...].astype(F32) + product + wide_ref[2:3, :]).astype(BF16)


def call(kernel, name, grid, ins, outs, scratch, flops, args):
    def spec(shape, rows):
        if rows in ("now", "past"):
            last = grid - 2
            place = (lambda i: jnp.minimum(i, last)) if rows == "now" else (lambda i: jnp.maximum(i - 1, 0))
            return pl.BlockSpec((shape[0] // (grid - 1),) + tuple(shape[1:]), lambda i: (place(i),) + (0,) * (len(shape) - 1))
        if rows == "any":
            return pl.BlockSpec(memory_space=pl.ANY)
        if rows == "smem":
            return pl.BlockSpec(memory_space=pltpu.SMEM)
        if rows == "half":
            return pl.BlockSpec((shape[0], shape[1] // 2), lambda i: (0, i))
        if rows is None:
            return pl.BlockSpec(shape, lambda i: (0,) * len(shape), pipeline_mode=pl.Buffered(1))
        return pl.BlockSpec((rows,) + tuple(shape[1:]), lambda i: (i,) + (0,) * (len(shape) - 1))

    results = [jax.ShapeDtypeStruct(shape, kind) for shape, kind, _ in outs]
    moved = sum(a.size * a.dtype.itemsize for a in list(args) + results)
    return pl.pallas_call(
        kernel,
        name=name,
        grid=(grid,),
        in_specs=[spec(a.shape, rows) for a, rows in zip(args, ins)],
        out_specs=[spec(shape, rows) for shape, _, rows in outs],
        out_shape=results,
        scratch_shapes=scratch,
        compiler_params=pltpu.CompilerParams(vmem_limit_bytes=VMEM_BYTES),
        cost_estimate=pl.CostEstimate(flops=flops, bytes_accessed=moved, transcendentals=0),
    )(*args)


def flags_of(lengths_row, keep_mask):
    count = keep_mask.shape[0]
    ends = jnp.cumsum(lengths_row)
    position = jnp.arange(count, dtype=jnp.int32)[:, None]

    def segment(at):
        return jnp.sum((at >= ends[None, :]).astype(jnp.int32), axis=1, keepdims=True)

    own = segment(position)
    columns = [keep_mask[:, None] != 0]
    for tap in range(KERNEL):
        source = position + (tap - KERNEL // 2) * DILATION
        columns.append((source >= 0) & (source < count) & (segment(source) == own))
    columns += [columns[0]] * (8 - len(columns))
    return jnp.concatenate([column.astype(F32) for column in columns], axis=1)


def with_small(weight, wide, narrow):
    rows, width = weight.shape
    first = -(-rows // 8) * 8
    out = jnp.pad(weight, ((0, first + 8 - rows), (0, 0)))
    for lane, group in ((0, wide), (128, narrow)):
        for k, item in enumerate(group):
            after = width - lane - item.shape[0]
            out = out + jnp.pad(item[None, :], ((first + k, 7 - k), (lane, after)))
    return out


def padded_rows(rows):
    return -(-rows // 8) * 8


def body(
    axes,
    inputs,
    lengths,
    keep_mask,
    cotangent,
    ln1_gain,
    ln1_bias,
    up_weight,
    up_bias,
    ln2_gain,
    ln2_bias,
    conv_weight,
    conv_bias,
    ln3_gain,
    ln3_bias,
    down_weight,
    down_bias,
):
    count, model = inputs.shape
    inner = up_weight.shape[1]
    dp, columns = axes[0][1], axes[1][1]
    chips = dp * columns
    place = jnp.stack([lax.axis_index(name) for name, _ in axes]).astype(jnp.int32)
    flags = flags_of(lengths[0], keep_mask)
    share, conv_share = model // (2 * chips), KERNEL * inner // (2 * chips)

    both_rows = padded_rows(share + conv_share)
    up_block = with_small(
        up_weight,
        (ln1_gain, ln1_bias, down_bias),
        (up_bias, ln2_gain, ln2_bias, conv_bias, ln3_gain, ln3_bias),
    )
    both_block = jnp.concatenate([down_weight.T, conv_weight.reshape(-1, inner)])
    both_block = jnp.pad(both_block, ((0, both_rows - share - conv_share), (0, 0)))
    up_one = jnp.stack(gather_stage(up_block, axes[1]))
    up_two = gather_stage(up_one, axes[0])
    name, size = axes[1]
    late_block = after(both_block, up_one)
    both_near = [both_block, swap(both_block, name, size, 1)]
    both_near += [swap(late_block, name, size, mask) for mask in range(2, size)]
    both_one = jnp.stack(after(tuple(both_near), *up_two))
    both_two = gather_stage(both_one, axes[0])
    up_pieces = core_stage([jnp.stack(up_two)], axes)

    block = 256
    steps = count // block
    wide_up = 2 * count * model * inner
    wide_conv = 2 * count * KERNEL * inner * inner
    padded = pltpu.VMEM((2, count + 2 * REACH, inner), BF16)

    act_one, up_full, wide, narrow = call(
        first_act_kernel, "first_act", steps, ("any", "any", block, "smem"),
        [((count, model), BF16, block), ((model, inner), BF16, None), ((8, model), F32, None), ((8, inner), F32, None)],
        [
            pltpu.VMEM((2 * chips,) + up_block.shape, BF16),
            pltpu.VMEM((model, inner), F32),
            pltpu.SemaphoreType.DMA((2 * chips,)),
        ],
        20 * count * model, (*up_pieces, after(inputs, both_one), place),
    )
    up_out, mid = call(
        up_kernel, "up", steps + 1, ("now", None, None, "past"),
        [((count, inner), F32, "past"), ((count, inner), BF16, "past")],
        [pltpu.VMEM((block, inner), F32)] * 2, wide_up, (act_one, up_full, narrow, flags),
    )
    both_pieces = core_stage(both_two[:1] + list(after(tuple(both_two[1:]), mid)), axes)
    any_of = ("any",) * len(both_pieces)
    top, low, conv_flat, down_full, top_sums, cot_sums = call(
        conv_kernel, "conv", steps + 1, any_of + (None, "now", None, "now", "smem"),
        [
            ((count, inner), BF16, "past"),
            ((count, inner), BF16, "past"),
            ((inner, KERNEL * inner), BF16, None),
            ((model, inner), BF16, None),
            ((24, inner), F32, None),
            ((8, model), F32, None),
        ],
        [
            padded,
            pltpu.VMEM((2 * chips,) + both_block.shape, BF16),
            pltpu.VMEM((KERNEL * inner, inner), F32),
            pltpu.VMEM((model, inner), F32),
            pltpu.VMEM((KERNEL * inner, inner), BF16),
            pltpu.VMEM((block, KERNEL * inner), BF16),
        ]
        + [pltpu.VMEM((block, inner), F32)] * 4
        + [pltpu.SemaphoreType.DMA((2 * chips,))],
        wide_conv + wide_up, (*both_pieces, mid, cotangent, narrow, flags, place),
    )
    both_kept, both_sent = call(
        weights_kernel, "weights", 1, (None, None, "any", "any", None, "smem"),
        [((dp, columns, both_rows, inner), BF16, "any")] * 2,
        [
            padded,
            pltpu.VMEM((KERNEL, inner, inner), F32),
            pltpu.VMEM((4, both_rows, inner), F32),
            pltpu.VMEM((count, inner), BF16),
            pltpu.VMEM((count, model), BF16),
            pltpu.VMEM((model, inner), F32),
            pltpu.VMEM((2, dp, columns, both_rows, inner), BF16),
            pltpu.SemaphoreType.DMA((2,)),
            pltpu.SemaphoreType.DMA((2,)),
        ],
        wide_conv + wide_up, (low, mid, top, cotangent, flags, place),
    )
    (output,) = call(
        output_kernel, "output", steps, (block, block, None, None),
        [((count, model), BF16, block)],
        [], wide_up, (inputs, after(top, both_sent), down_full, wide),
    )
    both = add_up(after(both_kept, output), [swap(both_sent, *axes[2], 1)])
    both_stage = scatter_stage(both, axes[0])
    up_low, mid_sums = call(
        mid_grad_kernel, "mid_grad", steps + 1, (None, None, "past", None, "now", "past"),
        [((count, inner), BF16, "past"), ((24, inner), F32, None)],
        [
            padded,
            pltpu.VMEM((block, KERNEL * inner), BF16),
            pltpu.VMEM((block, inner), F32),
            pltpu.VMEM((block, inner), F32),
        ],
        wide_conv, (after(low, both), conv_flat, up_out, narrow, flags, flags),
    )
    up_kept, up_sent = call(
        up_weight_kernel, "up_weight", 2, ("half", None, "smem"),
        [((dp, columns, share, inner), BF16, "any")] * 2,
        [
            pltpu.VMEM((model // 2, inner), F32),
            pltpu.VMEM((2, dp, columns, share, inner), BF16),
            pltpu.SemaphoreType.DMA((2,)),
        ],
        wide_up, (act_one, up_low, place),
    )
    up_grad = add_up(up_kept, [swap(up_sent, *axes[2], 1)])
    up_stage = scatter_stage(up_grad, axes[0])
    both = add_up(both_stage[0], [after(item, up_kept) for item in both_stage[1]])
    both_stage = scatter_stage(both, axes[1])
    input_grad, small_kept, small_sent = call(
        input_grad_kernel, "input_grad", steps + 1,
        ("now", None, "past", "past", None, None, None, None, "smem"),
        [((count, model), F32, "past")] + [((dp, columns, 16, 128), F32, "any")] * 2,
        [
            pltpu.VMEM((block, model), F32),
            pltpu.VMEM((block, model), F32),
            pltpu.VMEM((16, model), F32),
            pltpu.VMEM((8, model), F32),
            pltpu.VMEM((8, inner), F32),
            pltpu.VMEM((2, dp, columns, 16, 128), F32),
            pltpu.SemaphoreType.DMA((2,)),
        ],
        wide_up, (after(up_low, both, up_grad), up_full, inputs, cotangent, wide, top_sums, mid_sums, cot_sums, place),
    )
    up_arrived, both_arrived = after((tuple(up_stage[1]), tuple(both_stage[1])), small_kept)
    small = small_kept + swap(after(small_sent, *up_arrived, *both_arrived), *axes[2], 1)
    up_stage = scatter_stage(add_up(up_stage[0], up_arrived), axes[1])
    small_own = exact_stage(exact_stage(small, axes[0]), axes[1])
    both_own = add_up(both_stage[0], both_arrived)
    up_own = add_up(*up_stage)
    down_own = both_own[0:share]
    conv_own = both_own[share : share + conv_share]
    wide_row, narrow_row = up_weight.shape[0], conv_weight.shape[1]
    sums = [small_own[at, :wide_row] for at in range(2)]
    sums += [small_own[8 + at, :narrow_row] for at in range(6)]
    sums.append(small_own[2, :wide_row])
    return (output, input_grad, up_own, conv_own.reshape(conv_weight.shape), down_own.T) + tuple(sums)


def solution(mesh):
    rows, columns = mesh.shape["dp"], mesh.shape["fsdp"] // 2
    split = Mesh(mesh.devices.reshape(rows, columns, 2), ALL)
    axes = (("dp", rows), ("chip", columns), ("core", 2))
    by_row = P(ALL)
    by_second = P(None, ALL)
    in_specs = [by_row] * 16
    in_specs[10] = in_specs[14] = by_second
    out_specs = [by_row] * 14
    out_specs[3] = out_specs[4] = by_second
    return jax.shard_map(
        functools.partial(body, axes),
        mesh=split,
        in_specs=tuple(in_specs),
        out_specs=tuple(out_specs),
        check_vma=False,
    )
```

```python
import functools

import jax
import jax.numpy as jnp
from jax import lax
from jax.experimental import pallas as pl
from jax.experimental.pallas import tpu as pltpu
from jax.sharding import Mesh
from jax.sharding import PartitionSpec as P

KERNEL = 5
DILATION = 8
REACH = KERNEL // 2 * DILATION
ALL = ("dp", "chip", "core")
F32 = jnp.float32
BF16 = jnp.bfloat16
TANH_ONE = 0.7978845608028654
TANH_THREE = TANH_ONE * 0.044715
ROWS = 32
VMEM_MIB = {"first_act": 24, "up": 14, "conv": 40, "weights": 44, "mid_grad": 24, "up_weight": 30, "input_grad": 20, "output": 12}


def swap(array, axis, size, mask):
    return lax.ppermute(array, axis, [(k, k ^ mask) for k in range(size)])


def after(value, *others):
    return lax.optimization_barrier((value, *others))[0]


def gather_stage(block, axis):
    name, size = axis
    return [block] + [swap(block, name, size, mask) for mask in range(1, size)]


def core_stage(pieces, axes):
    return pieces + [swap(piece, axes[2][0], axes[2][1], 1) for piece in pieces]


def scatter_stage(total, axis):
    name, size = axis
    arrived = [swap(total[mask].astype(BF16), name, size, mask) for mask in range(1, size)]
    return total[0], arrived


def add_up(kept, arrived):
    total = kept.astype(F32)
    for item in arrived:
        total = total + item.astype(F32)
    return total


def exact_stage(total, axis):
    name, size = axis
    return total[0] + sum(swap(total[mask], name, size, mask) for mask in range(1, size))


def norm(z, width):
    center = z - jnp.sum(z, axis=1, keepdims=True) * (1.0 / width)
    scale = lax.rsqrt(jnp.sum(center * center, axis=1, keepdims=True) * (1.0 / width) + 1e-05)
    return center * scale, scale


def pipelined(product, rest, keep):
    step, last = pl.program_id(0), pl.num_programs(0) - 1

    @pl.when(step == 0)
    def _():
        product()
        keep()

    @pl.when((step > 0) & (step < last))
    def _():
        product()
        rest()
        keep()

    @pl.when(step == last)
    def _():
        rest()


def half_gelu(h):
    q = h * h
    t = jnp.tanh(h * (2.0 * TANH_ONE + 8.0 * TANH_THREE * q))
    return q, t, 1.0 + t


def double_slope(h, q, t, one_t):
    return one_t * (1.0 + (1.0 - t) * (h * (2.0 * TANH_ONE + 24.0 * TANH_THREE * q)))


def back_parts(hat, scale, half_gain, slope2, grad, width):
    by_sum = slope2 * grad
    by_gain = by_sum * hat
    by_hat = by_sum * half_gain
    first = jnp.sum(by_hat, axis=1, keepdims=True) * (scale * (1.0 / width))
    second = jnp.sum(by_hat * hat, axis=1, keepdims=True) * (scale * (1.0 / width))
    return scale * by_hat - first - hat * second, by_gain, by_sum


def fold(value):
    return sum(value[k : k + 8] for k in range(0, value.shape[0], 8))


def chunks(count, body, unroll=4):
    def step(k, carry):
        body(pl.multiple_of(k * ROWS, ROWS))
        return carry

    lax.fori_loop(0, count // ROWS, step, 0, unroll=unroll)


def dot(left, right, left_dim=1, right_dim=0):
    return lax.dot_general(
        left, right, (((left_dim,), (right_dim,)), ((), ())), preferred_element_type=F32
    )


def piece_copies(pieces, place_ref, hold_ref, semaphores):
    half = len(pieces) // 2
    columns = pieces[0].shape[0]
    copies = []
    for c in range(2):
        for o in range(half):
            for i in range(columns):
                chip = (place_ref[0] ^ o) * columns + (place_ref[1] ^ i)
                target = hold_ref.at[2 * chip + (place_ref[2] ^ c)]
                copies.append(pltpu.make_async_copy(pieces[c * half + o].at[i], target, semaphores.at[len(copies)]))
    return copies


def first_act_kernel(
    own_pieces, other_pieces, x_ref, place_ref,
    act_ref, up_ref, down_ref, wide_ref, narrow_ref, hold_ref, up_wide_ref, down_wide_ref, semaphores,
):
    block, width = x_ref.shape

    @pl.when(pl.program_id(0) == 0)
    def _():
        parts = [piece.at[o] for piece in (own_pieces, other_pieces) for o in range(piece.shape[0])]
        copies = piece_copies(parts, place_ref, hold_ref, semaphores)
        for copy in copies:
            copy.start()
        for copy in copies:
            copy.wait()
        devices = hold_ref.shape[0]
        share, of_narrow = width // devices, narrow_ref.shape[1] // devices
        for k in range(devices):
            item = hold_ref[k].astype(F32)
            small = item[item.shape[0] - 8 :, :]
            wide_ref[:, k * share : (k + 1) * share] = small[:, 0:share]
            narrow_ref[:, k * of_narrow : (k + 1) * of_narrow] = small[:, 128 : 128 + of_narrow]
            up_wide_ref[k * share : (k + 1) * share, :] = item[0:share, :]
            down_wide_ref[k * share : (k + 1) * share, :] = item[share : 2 * share, :]
        up_ref[...] = up_wide_ref[...].astype(BF16)
        down_ref[...] = down_wide_ref[...].astype(BF16)

    gain, bias = 0.5 * wide_ref[0:1, :], 0.5 * wide_ref[1:2, :]

    def body(at):
        hat, _ = norm(x_ref[pl.ds(at, ROWS), :].astype(F32), width)
        h = hat * gain + bias
        act_ref[pl.ds(at, ROWS), :] = (h * half_gelu(h)[2]).astype(BF16)

    chunks(block, body)


def up_kernel(act_ref, weight_ref, narrow_ref, flags_ref, out_ref, mid_ref, z_ref, next_ref):
    block, width = out_ref.shape

    def product():
        next_ref[...] = dot(act_ref[...], weight_ref[...])

    def keep():
        z_ref[...] = next_ref[...]

    def rest():
        shift, gain, bias = narrow_ref[0:1, :], 0.5 * narrow_ref[1:2, :], 0.5 * narrow_ref[2:3, :]
        for at in range(0, block, ROWS):
            rows = slice(at, at + ROWS)
            z = z_ref[rows, :] + shift
            out_ref[rows, :] = z
            hat, _ = norm(z, width)
            h = hat * gain + bias
            mid_ref[rows, :] = (h * half_gelu(h)[2] * flags_ref[rows, 0:1]).astype(BF16)

    pipelined(product, rest, keep)


def fill_padded(padded_ref, source_ref):
    count, width = source_ref.shape
    padded_ref[0, 0:REACH, :] = jnp.zeros((REACH, width), BF16)
    padded_ref[0, count + REACH : count + 2 * REACH, :] = jnp.zeros((REACH, width), BF16)
    padded_ref[0, REACH : count + REACH, :] = source_ref[...]
    padded_ref[1, 0 : count + REACH, :] = padded_ref[0, DILATION : count + REACH + DILATION, :]


def shifted(padded_ref, flags, start, block, tap):
    which, at = tap % 2, start + tap // 2 * (2 * DILATION)
    if not isinstance(at, int):
        at = pl.multiple_of(at, 2 * DILATION)
    rows = padded_ref[which, pl.ds(at, block), :]
    if tap != KERNEL // 2:
        rows = rows * flags[:, tap + 1 : tap + 2]
    return rows


def conv_kernel(*refs):
    pieces, rest_refs = refs[: len(refs) - 22], refs[len(refs) - 22 :]
    (
        mid_ref, down_ref, cot_ref, narrow_ref, now_flags_ref, place_ref,
        top_ref, low_ref, flat_hbm, sums_ref, wide_sums_ref,
        padded_ref, hold_ref, wide_weight_ref, weight_ref, flat_ref, taps_ref,
        out_ref, grad_ref, next_out_ref, next_grad_ref, semaphores,
    ) = rest_refs
    step = pl.program_id(0)
    block, width = out_ref.shape
    devices = hold_ref.shape[0]
    share = width // devices
    flat_copy = pltpu.make_async_copy(flat_ref, flat_hbm, semaphores.at[devices])

    @pl.when(step == 0)
    def _():
        copies = piece_copies(pieces, place_ref, hold_ref, semaphores)
        for copy in copies:
            copy.start()
        fill_padded(padded_ref, mid_ref)
        sums_ref[...] = jnp.zeros_like(sums_ref)
        wide_sums_ref[...] = jnp.zeros_like(wide_sums_ref)
        for copy in copies:
            copy.wait()
        for tap in range(KERNEL):
            for k in range(devices):
                item = hold_ref[k].astype(F32)
                wide_weight_ref[tap % 2, k * share : (k + 1) * share, :] = item[tap * share : (tap + 1) * share, :]
            part = wide_weight_ref[tap % 2].astype(BF16)
            weight_ref[tap * width : (tap + 1) * width, :] = part
            flat_ref[:, tap * width : (tap + 1) * width] = part
        flat_copy.start()

    def product():
        start = jnp.minimum(step, pl.num_programs(0) - 2) * block
        flags = now_flags_ref[...].astype(BF16)
        for tap in range(KERNEL):
            taps_ref[:, tap * width : (tap + 1) * width] = shifted(padded_ref, flags, start, block, tap)
        next_out_ref[...] = dot(taps_ref[...], weight_ref[...])
        next_grad_ref[...] = dot(cot_ref[...], down_ref[...])
        total = wide_sums_ref[...]
        for at in range(0, block, ROWS):
            total += fold(cot_ref[at : at + ROWS, :].astype(F32))
        wide_sums_ref[...] = total

    def keep():
        out_ref[...] = next_out_ref[...]
        grad_ref[...] = next_grad_ref[...]

    def rest():
        shift, gain, bias = narrow_ref[3:4, :], 0.5 * narrow_ref[4:5, :], 0.5 * narrow_ref[5:6, :]
        totals = [sums_ref[8 * k : 8 * k + 8, :] for k in range(3)]
        for at in range(0, block, ROWS):
            rows = slice(at, at + ROWS)
            hat, scale = norm(out_ref[rows, :] + shift, width)
            h = hat * gain + bias
            q, t, one_t = half_gelu(h)
            top_ref[rows, :] = (h * one_t).astype(BF16)
            slope2 = double_slope(h, q, t, one_t)
            back, by_gain, by_sum = back_parts(hat, scale, gain, slope2, grad_ref[rows, :], width)
            low_ref[rows, :] = back.astype(BF16)
            for k, part in enumerate((by_gain, by_sum, back)):
                totals[k] += fold(part)
        for k in range(3):
            sums_ref[8 * k : 8 * k + 8, :] = totals[k]

    pipelined(product, rest, keep)

    @pl.when(step == pl.num_programs(0) - 1)
    def _():
        flat_copy.wait()


def hand_out(place_ref, device, columns, ready_ref, rows, part):
    chip = device // 2
    m, n = (chip // columns) ^ place_ref[0], (chip % columns) ^ place_ref[1]
    which = (device % 2) ^ place_ref[2]
    if isinstance(rows, int):
        ready_ref[which, m, n, rows] = part.astype(ready_ref.dtype)
    else:
        ready_ref[which, m, n, rows, 0 : part.shape[1]] = part.astype(ready_ref.dtype)


def send_out(ready_ref, kept_hbm, sent_hbm, semaphores):
    copies = [
        pltpu.make_async_copy(ready_ref.at[k], target, semaphores.at[k])
        for k, target in enumerate((kept_hbm, sent_hbm))
    ]
    for copy in copies:
        copy.start()
    for copy in copies:
        copy.wait()


def weights_kernel(
    low_ref, mid_ref, flags_ref, place_ref, kept_hbm, sent_hbm,
    padded_ref, taps_ref, total_ref, row_ref, ready_ref, out_semaphores,
):
    count, width = mid_ref.shape
    columns = ready_ref.shape[2]
    devices = 2 * ready_ref.shape[1] * columns
    share = width // devices
    fill_padded(padded_ref, low_ref)
    flags = flags_ref[...].astype(BF16)
    for tap in range(KERNEL):
        taps_ref[:, tap * width : (tap + 1) * width] = shifted(padded_ref, flags, 0, count, KERNEL - 1 - tap)
    total_ref[...] = dot(mid_ref[...].T, taps_ref[...])
    row_ref[...] = jnp.zeros_like(row_ref)
    for device in range(devices):
        slot = device % row_ref.shape[0]
        for tap in range(KERNEL):
            part = total_ref[device * share : (device + 1) * share, tap * width : (tap + 1) * width]
            row_ref[slot, tap * share : (tap + 1) * share, :] = part
        hand_out(place_ref, device, columns, ready_ref, slice(None), row_ref[slot])
    send_out(ready_ref, kept_hbm, sent_hbm, out_semaphores)


def up_weight_kernel(
    act_ref, cot_ref, low_ref, top_ref, place_ref, kept_hbm, sent_hbm, total_ref, ready_ref, out_semaphores
):
    step, steps = pl.program_id(0), pl.num_programs(0)
    share = ready_ref.shape[4]
    devices = total_ref.shape[0] // share

    def part_of(group, left_ref, right_ref):
        total_ref[...] = dot(left_ref[...], right_ref[...], 0, 0)
        first = lax.rem(step, steps // 2) * devices
        for k in range(devices):
            part = total_ref[k * share : (k + 1) * share, :]
            hand_out(place_ref, first + k, ready_ref.shape[2], ready_ref, group, part)

    @pl.when(step < steps // 2)
    def _():
        part_of(0, act_ref, low_ref)

    @pl.when(step >= steps // 2)
    def _():
        part_of(1, cot_ref, top_ref)

    @pl.when(step == steps - 1)
    def _():
        send_out(ready_ref, kept_hbm, sent_hbm, out_semaphores)


def mid_grad_kernel(
    low_ref, flat_ref, up_out_ref, narrow_ref, now_flags_ref, flags_ref,
    up_low_ref, sums_ref,
    padded_ref, taps_ref, grad_ref, next_ref,
):
    step = pl.program_id(0)
    block, width = up_out_ref.shape

    @pl.when(step == 0)
    def _():
        fill_padded(padded_ref, low_ref)
        sums_ref[...] = jnp.zeros_like(sums_ref)

    def product():
        start = jnp.minimum(step, pl.num_programs(0) - 2) * block
        flags = now_flags_ref[...].astype(BF16)
        for tap in range(KERNEL):
            taps_ref[:, tap * width : (tap + 1) * width] = shifted(padded_ref, flags, start, block, KERNEL - 1 - tap)
        next_ref[...] = dot(taps_ref[...], flat_ref[...], 1, 1)

    def keep():
        grad_ref[...] = next_ref[...]

    def rest():
        gain, bias = 0.5 * narrow_ref[1:2, :], 0.5 * narrow_ref[2:3, :]
        totals = [sums_ref[8 * k : 8 * k + 8, :] for k in range(3)]
        for at in range(0, block, ROWS):
            rows = slice(at, at + ROWS)
            hat, scale = norm(up_out_ref[rows, :], width)
            h = hat * gain + bias
            slope2 = double_slope(h, *half_gelu(h))
            grad = grad_ref[rows, :] * flags_ref[rows, 0:1]
            back, by_gain, by_sum = back_parts(hat, scale, gain, slope2, grad, width)
            up_low_ref[rows, :] = back.astype(BF16)
            for k, part in enumerate((by_gain, by_sum, back)):
                totals[k] += fold(part)
        for k in range(3):
            sums_ref[8 * k : 8 * k + 8, :] = totals[k]

    pipelined(product, rest, keep)


def input_grad_kernel(
    up_low_ref, weight_ref, x_ref, cot_ref, wide_ref, top_sums_ref, mid_sums_ref, cot_sums_ref, place_ref,
    out_ref, kept_hbm, sent_hbm,
    grad_ref, next_ref, sums_ref, wide_row_ref, narrow_row_ref, ready_ref, out_semaphores,
):
    step, steps = pl.program_id(0), pl.num_programs(0)
    block, width = out_ref.shape

    @pl.when(step == 0)
    def _():
        sums_ref[...] = jnp.zeros_like(sums_ref)

    def product():
        next_ref[...] = dot(up_low_ref[...], weight_ref[...], 1, 1)

    def keep():
        grad_ref[...] = next_ref[...]

    def rest():
        gain, bias = 0.5 * wide_ref[0:1, :], 0.5 * wide_ref[1:2, :]
        by_gains, by_sums = sums_ref[0:8, :], sums_ref[8:16, :]
        for at in range(0, block, ROWS):
            rows = slice(at, at + ROWS)
            hat, scale = norm(x_ref[rows, :].astype(F32), width)
            h = hat * gain + bias
            slope2 = double_slope(h, *half_gelu(h))
            back, by_gain, by_sum = back_parts(hat, scale, gain, slope2, grad_ref[rows, :], width)
            out_ref[rows, :] = cot_ref[rows, :].astype(F32) + back
            by_gains += fold(by_gain)
            by_sums += fold(by_sum)
        sums_ref[0:8, :] = by_gains
        sums_ref[8:16, :] = by_sums

    pipelined(product, rest, keep)

    @pl.when(step == steps - 1)
    def _():
        def row(ref, k):
            return jnp.sum(ref[8 * k : 8 * k + 8, :], axis=0, keepdims=True)

        wide_row_ref[...] = jnp.zeros_like(wide_row_ref)
        narrow_row_ref[...] = jnp.zeros_like(narrow_row_ref)
        for at, (ref, k, factor) in enumerate(((sums_ref, 0, 0.5), (sums_ref, 1, 0.5), (cot_sums_ref, 0, 1.0))):
            wide_row_ref[at : at + 1, :] = factor * row(ref, k)
        rows = (
            (mid_sums_ref, 2, 1.0),
            (mid_sums_ref, 0, 0.5),
            (mid_sums_ref, 1, 0.5),
            (top_sums_ref, 2, 1.0),
            (top_sums_ref, 0, 0.5),
            (top_sums_ref, 1, 0.5),
        )
        for at, (ref, k, factor) in enumerate(rows):
            narrow_row_ref[at : at + 1, :] = factor * row(ref, k)
        columns = ready_ref.shape[2]
        devices = 2 * ready_ref.shape[1] * columns
        wide, narrow = width // devices, narrow_row_ref.shape[1] // devices
        ready_ref[...] = jnp.zeros_like(ready_ref)
        for device in range(devices):
            wide_part = wide_row_ref[:, device * wide : (device + 1) * wide]
            narrow_part = narrow_row_ref[:, device * narrow : (device + 1) * narrow]
            hand_out(place_ref, device, columns, ready_ref, slice(0, 8), wide_part)
            hand_out(place_ref, device, columns, ready_ref, slice(8, 16), narrow_part)
        send_out(ready_ref, kept_hbm, sent_hbm, out_semaphores)


def output_kernel(x_ref, top_ref, weight_ref, wide_ref, out_ref):
    product = dot(top_ref[...], weight_ref[...], 1, 1)
    out_ref[...] = (x_ref[...].astype(F32) + product + wide_ref[2:3, :]).astype(BF16)


def call(kernel, name, grid, ins, outs, scratch, flops, args):
    def spec(shape, rows):
        if rows in ("now", "past"):
            last = grid - 2
            place = (lambda i: jnp.minimum(i, last)) if rows == "now" else (lambda i: jnp.maximum(i - 1, 0))
            return pl.BlockSpec((shape[0] // (grid - 1),) + tuple(shape[1:]), lambda i: (place(i),) + (0,) * (len(shape) - 1))
        if rows == "any":
            return pl.BlockSpec(memory_space=pl.ANY)
        if rows == "smem":
            return pl.BlockSpec(memory_space=pltpu.SMEM)
        if rows in ("early half", "late half"):
            start = 0 if rows == "early half" else grid // 2
            return pl.BlockSpec((shape[0], shape[1] // 2), lambda i: (0, jnp.clip(i - start, 0, 1)))
        if rows is None:
            return pl.BlockSpec(shape, lambda i: (0,) * len(shape), pipeline_mode=pl.Buffered(1))
        return pl.BlockSpec((rows,) + tuple(shape[1:]), lambda i: (i,) + (0,) * (len(shape) - 1))

    results = [jax.ShapeDtypeStruct(shape, kind) for shape, kind, _ in outs]
    moved = sum(a.size * a.dtype.itemsize for a in list(args) + results) if flops > 1 else 1
    return pl.pallas_call(
        kernel,
        name=name,
        grid=(grid,),
        in_specs=[spec(a.shape, rows) for a, rows in zip(args, ins)],
        out_specs=[spec(shape, rows) for shape, _, rows in outs],
        out_shape=results,
        scratch_shapes=scratch,
        compiler_params=pltpu.CompilerParams(vmem_limit_bytes=VMEM_MIB[name] * 2**20),
        cost_estimate=pl.CostEstimate(flops=flops, bytes_accessed=moved, transcendentals=0),
    )(*args)


def flags_of(lengths_row, keep_mask):
    count = keep_mask.shape[0]
    ends = jnp.cumsum(lengths_row)
    position = jnp.arange(count, dtype=jnp.int32)[:, None]

    def segment(at):
        return jnp.sum((at >= ends[None, :]).astype(jnp.int32), axis=1, keepdims=True)

    own = segment(position)
    columns = [keep_mask[:, None] != 0]
    for tap in range(KERNEL):
        source = position + (tap - KERNEL // 2) * DILATION
        columns.append((source >= 0) & (source < count) & (segment(source) == own))
    columns += [columns[0]] * (8 - len(columns))
    return jnp.concatenate([column.astype(F32) for column in columns], axis=1)


def with_small(weight, wide, narrow):
    rows, width = weight.shape
    first = -(-rows // 8) * 8
    out = jnp.pad(weight, ((0, first + 8 - rows), (0, 0)))
    for lane, group in ((0, wide), (128, narrow)):
        for k, item in enumerate(group):
            after = width - lane - item.shape[0]
            out = out + jnp.pad(item[None, :], ((first + k, 7 - k), (lane, after)))
    return out


def padded_rows(rows):
    return -(-rows // 8) * 8


def body(
    axes,
    inputs,
    lengths,
    keep_mask,
    cotangent,
    ln1_gain,
    ln1_bias,
    up_weight,
    up_bias,
    ln2_gain,
    ln2_bias,
    conv_weight,
    conv_bias,
    ln3_gain,
    ln3_bias,
    down_weight,
    down_bias,
):
    count, model = inputs.shape
    inner = up_weight.shape[1]
    dp, columns = axes[0][1], axes[1][1]
    chips = dp * columns
    place = jnp.stack([lax.axis_index(name) for name, _ in axes]).astype(jnp.int32)
    flags = flags_of(lengths[0], keep_mask)
    share, conv_share = model // (2 * chips), KERNEL * inner // (2 * chips)

    conv_rows = padded_rows(conv_share)
    up_block = with_small(
        jnp.concatenate([up_weight, down_weight.T]),
        (ln1_gain, ln1_bias, down_bias),
        (up_bias, ln2_gain, ln2_bias, conv_bias, ln3_gain, ln3_bias),
    )
    conv_block = jnp.pad(conv_weight.reshape(-1, inner), ((0, conv_rows - conv_share), (0, 0)))
    up_one = jnp.stack(gather_stage(up_block, axes[1]))
    up_two = gather_stage(up_one, axes[0])
    name, size = axes[1]
    late_block = after(conv_block, up_one)
    conv_near = [conv_block, swap(conv_block, name, size, 1)]
    conv_near += [swap(late_block, name, size, mask) for mask in range(2, size)]
    conv_one = jnp.stack(after(tuple(conv_near), *up_two))
    conv_two = gather_stage(conv_one, axes[0])
    up_pieces = core_stage([jnp.stack(after(tuple(up_two), *conv_near))], axes)

    block = 256
    steps = count // block
    wide_up = 2 * count * model * inner
    wide_conv = 2 * count * KERNEL * inner * inner
    padded = pltpu.VMEM((2, count + 2 * REACH, inner), BF16)

    act_one, up_full, down_full, wide, narrow = call(
        first_act_kernel, "first_act", steps, ("any", "any", block, "smem"),
        [
            ((count, model), BF16, block),
            ((model, inner), BF16, None),
            ((model, inner), BF16, None),
            ((8, model), F32, None),
            ((8, inner), F32, None),
        ],
        [
            pltpu.VMEM((2 * chips,) + up_block.shape, BF16),
            pltpu.VMEM((model, inner), F32),
            pltpu.VMEM((model, inner), F32),
            pltpu.SemaphoreType.DMA((2 * chips,)),
        ],
        20 * count * model, (*up_pieces, inputs, after(place, conv_one)),
    )
    up_out, mid = call(
        up_kernel, "up", steps + 1, ("now", None, None, "past"),
        [((count, inner), F32, "past"), ((count, inner), BF16, "past")],
        [pltpu.VMEM((block, inner), F32)] * 2, wide_up, (act_one, up_full, narrow, flags),
    )
    conv_pieces = core_stage(conv_two[:1] + list(after(tuple(conv_two[1:]), mid)), axes)
    top, low, conv_flat, top_sums, cot_sums = call(
        conv_kernel, "conv", steps + 1, ("any",) * len(conv_pieces) + (None, None, "now", None, "now", "smem"),
        [
            ((count, inner), BF16, "past"),
            ((count, inner), BF16, "past"),
            ((inner, KERNEL * inner), BF16, "any"),
            ((24, inner), F32, None),
            ((8, model), F32, None),
        ],
        [
            padded,
            pltpu.VMEM((2 * chips,) + conv_block.shape, BF16),
            pltpu.VMEM((2, inner, inner), F32),
            pltpu.VMEM((KERNEL * inner, inner), BF16),
            pltpu.VMEM((inner, KERNEL * inner), BF16),
            pltpu.VMEM((block, KERNEL * inner), BF16),
        ]
        + [pltpu.VMEM((block, inner), F32)] * 4
        + [pltpu.SemaphoreType.DMA((2 * chips + 1,))],
        wide_conv + wide_up, (*conv_pieces, mid, down_full, cotangent, narrow, flags, place),
    )
    conv_kept, conv_sent = call(
        weights_kernel, "weights", 1, (None, None, None, "smem"),
        [((dp, columns, conv_rows, inner), BF16, "any")] * 2,
        [
            padded,
            pltpu.VMEM((count, KERNEL * inner), BF16),
            pltpu.VMEM((inner, KERNEL * inner), F32),
            pltpu.VMEM((4, conv_rows, inner), F32),
            pltpu.VMEM((2, dp, columns, conv_rows, inner), BF16),
            pltpu.SemaphoreType.DMA((2,)),
        ],
        wide_conv, (low, mid, flags, place),
    )
    (output,) = call(
        output_kernel, "output", steps, (block, block, None, None),
        [((count, model), BF16, block)],
        [], wide_up, (inputs, top, down_full, after(wide, conv_sent)),
    )
    conv_grad = add_up(after(conv_kept, output), [swap(conv_sent, *axes[2], 1)])
    conv_stage = scatter_stage(conv_grad, axes[0])
    up_low, mid_sums = call(
        mid_grad_kernel, "mid_grad", steps + 1, (None, None, "past", None, "now", "past"),
        [((count, inner), BF16, "past"), ((24, inner), F32, None)],
        [
            padded,
            pltpu.VMEM((block, KERNEL * inner), BF16),
            pltpu.VMEM((block, inner), F32),
            pltpu.VMEM((block, inner), F32),
        ],
        wide_conv, (low, conv_flat, up_out, after(narrow, conv_grad), flags, flags),
    )
    up_kept, up_sent = call(
        up_weight_kernel, "up_weight", 4, ("early half", "late half", None, None, "smem"),
        [((dp, columns, 2, share, inner), BF16, "any")] * 2,
        [
            pltpu.VMEM((model // 2, inner), F32),
            pltpu.VMEM((2, dp, columns, 2, share, inner), BF16),
            pltpu.SemaphoreType.DMA((2,)),
        ],
        1, (act_one, cotangent, up_low, top, place),
    )
    conv_arrived = after(tuple(conv_stage[1]), up_kept)
    up_grad = add_up(up_kept, [swap(after(up_sent, *conv_arrived), *axes[2], 1)])
    up_stage = scatter_stage(up_grad, axes[0])
    conv_grad = add_up(conv_stage[0], conv_arrived)
    conv_stage = scatter_stage(conv_grad, axes[1])
    input_grad, small_kept, small_sent = call(
        input_grad_kernel, "input_grad", steps + 1,
        ("now", None, "past", "past", None, None, None, None, "smem"),
        [((count, model), F32, "past")] + [((dp, columns, 16, 128), F32, "any")] * 2,
        [
            pltpu.VMEM((block, model), F32),
            pltpu.VMEM((block, model), F32),
            pltpu.VMEM((16, model), F32),
            pltpu.VMEM((8, model), F32),
            pltpu.VMEM((8, inner), F32),
            pltpu.VMEM((2, dp, columns, 16, 128), F32),
            pltpu.SemaphoreType.DMA((2,)),
        ],
        wide_up,
        (up_low, up_full, inputs, cotangent, wide, top_sums, mid_sums, cot_sums, after(place, conv_grad, up_grad)),
    )
    up_arrived, conv_arrived = after((tuple(up_stage[1]), tuple(conv_stage[1])), small_kept)
    small = small_kept + swap(after(small_sent, *up_arrived, *conv_arrived), *axes[2], 1)
    up_stage = scatter_stage(add_up(up_stage[0], up_arrived), axes[1])
    small_own = exact_stage(exact_stage(small, axes[0]), axes[1])
    conv_own = add_up(conv_stage[0], conv_arrived)[0:conv_share]
    up_own, down_own = add_up(*up_stage)
    wide_row, narrow_row = up_weight.shape[0], conv_weight.shape[1]
    sums = [small_own[at, :wide_row] for at in range(2)]
    sums += [small_own[8 + at, :narrow_row] for at in range(6)]
    sums.append(small_own[2, :wide_row])
    return (output, input_grad, up_own, conv_own.reshape(conv_weight.shape), down_own.T) + tuple(sums)


def solution(mesh):
    rows, columns = mesh.shape["dp"], mesh.shape["fsdp"] // 2
    split = Mesh(mesh.devices.reshape(rows, columns, 2), ALL)
    axes = (("dp", rows), ("chip", columns), ("core", 2))
    by_row = P(ALL)
    by_second = P(None, ALL)
    in_specs = [by_row] * 16
    in_specs[10] = in_specs[14] = by_second
    out_specs = [by_row] * 14
    out_specs[3] = out_specs[4] = by_second
    return jax.shard_map(
        functools.partial(body, axes),
        mesh=split,
        in_specs=tuple(in_specs),
        out_specs=tuple(out_specs),
        check_vma=False,
    )
```

```python
import functools

import jax
import jax.numpy as jnp
from jax import lax
from jax.experimental import pallas as pl
from jax.experimental.pallas import tpu as pltpu
from jax.sharding import Mesh
from jax.sharding import PartitionSpec as P

KERNEL = 5
DILATION = 8
REACH = KERNEL // 2 * DILATION
ALL = ("dp", "chip", "core")
F32 = jnp.float32
BF16 = jnp.bfloat16
TANH_ONE = 0.7978845608028654
TANH_THREE = TANH_ONE * 0.044715
ROWS = 32
VMEM_MIB = {"first_act": 61, "up": 61, "conv": 61, "weights": 44, "mid_grad": 24, "up_weight": 30, "input_grad": 20, "output": 12}


def swap(array, axis, size, mask):
    return lax.ppermute(array, axis, [(k, k ^ mask) for k in range(size)])


def after(value, *others):
    return lax.optimization_barrier((value, *others))[0]


def gather_stage(block, axis):
    name, size = axis
    return [block] + [swap(block, name, size, mask) for mask in range(1, size)]


def core_stage(pieces, axes):
    return pieces + [swap(piece, axes[2][0], axes[2][1], 1) for piece in pieces]


def scatter_stage(total, axis):
    name, size = axis
    arrived = [swap(total[mask].astype(BF16), name, size, mask) for mask in range(1, size)]
    return total[0], arrived


def add_up(kept, arrived):
    total = kept.astype(F32)
    for item in arrived:
        total = total + item.astype(F32)
    return total


def exact_stage(total, axis):
    name, size = axis
    return total[0] + sum(swap(total[mask], name, size, mask) for mask in range(1, size))


def norm(z, width):
    center = z - jnp.sum(z, axis=1, keepdims=True) * (1.0 / width)
    scale = lax.rsqrt(jnp.sum(center * center, axis=1, keepdims=True) * (1.0 / width) + 1e-05)
    return center * scale, scale


def pipelined(product, rest, keep):
    step, last = pl.program_id(0), pl.num_programs(0) - 1

    @pl.when(step == 0)
    def _():
        product()
        keep()

    @pl.when((step > 0) & (step < last))
    def _():
        product()
        rest()
        keep()

    @pl.when(step == last)
    def _():
        rest()


def half_gelu(h):
    q = h * h
    t = jnp.tanh(h * (2.0 * TANH_ONE + 8.0 * TANH_THREE * q))
    return q, t, 1.0 + t


def double_slope(h, q, t, one_t):
    return one_t * (1.0 + (1.0 - t) * (h * (2.0 * TANH_ONE + 24.0 * TANH_THREE * q)))


def back_parts(hat, scale, half_gain, slope2, grad, width):
    by_sum = slope2 * grad
    by_gain = by_sum * hat
    by_hat = by_sum * half_gain
    first = jnp.sum(by_hat, axis=1, keepdims=True) * (scale * (1.0 / width))
    second = jnp.sum(by_hat * hat, axis=1, keepdims=True) * (scale * (1.0 / width))
    return scale * by_hat - first - hat * second, by_gain, by_sum


def fold(value):
    return sum(value[k : k + 8] for k in range(0, value.shape[0], 8))


def dot(left, right, left_dim=1, right_dim=0):
    return lax.dot_general(
        left, right, (((left_dim,), (right_dim,)), ((), ())), preferred_element_type=F32
    )


def piece_copies(pieces, place_ref, hold_ref, semaphores):
    half = len(pieces) // 2
    columns = pieces[0].shape[0]
    copies = []
    for c in range(2):
        for o in range(half):
            for i in range(columns):
                chip = (place_ref[0] ^ o) * columns + (place_ref[1] ^ i)
                target = hold_ref.at[2 * chip + (place_ref[2] ^ c)]
                copies.append(pltpu.make_async_copy(pieces[c * half + o].at[i], target, semaphores.at[len(copies)]))
    return copies


def up_kernel(
    own_pieces, other_pieces, x_ref, flags_ref, place_ref,
    act_ref, up_ref, down_ref, wide_ref, narrow_ref, out_ref, mid_ref,
    hold_ref, up_wide_ref, down_wide_ref, z_ref, next_ref, semaphores,
):
    block, width = x_ref.shape
    inner = z_ref.shape[1]

    @pl.when(pl.program_id(0) == 0)
    def _():
        parts = [piece.at[o] for piece in (own_pieces, other_pieces) for o in range(piece.shape[0])]
        copies = piece_copies(parts, place_ref, hold_ref, semaphores)
        for copy in copies:
            copy.start()
        for copy in copies:
            copy.wait()
        devices = hold_ref.shape[0]
        share, of_narrow = width // devices, narrow_ref.shape[1] // devices
        for k in range(devices):
            item = hold_ref[k].astype(F32)
            small = item[item.shape[0] - 8 :, :]
            wide_ref[:, k * share : (k + 1) * share] = small[:, 0:share]
            narrow_ref[:, k * of_narrow : (k + 1) * of_narrow] = small[:, 128 : 128 + of_narrow]
            up_wide_ref[k * share : (k + 1) * share, :] = item[0:share, :]
            down_wide_ref[k * share : (k + 1) * share, :] = item[share : 2 * share, :]
        up_ref[...] = up_wide_ref[...].astype(BF16)
        down_ref[...] = down_wide_ref[...].astype(BF16)

    def product():
        gain, bias = 0.5 * wide_ref[0:1, :], 0.5 * wide_ref[1:2, :]
        for at in range(0, block, ROWS):
            rows = slice(at, at + ROWS)
            hat, _ = norm(x_ref[rows, :].astype(F32), width)
            h = hat * gain + bias
            act_ref[rows, :] = (h * half_gelu(h)[2]).astype(BF16)
        next_ref[...] = dot(act_ref[...], up_ref[...])

    def keep():
        z_ref[...] = next_ref[...]

    def rest():
        shift, gain, bias = narrow_ref[0:1, :], 0.5 * narrow_ref[1:2, :], 0.5 * narrow_ref[2:3, :]
        for at in range(0, block, ROWS):
            rows = slice(at, at + ROWS)
            z = z_ref[rows, :] + shift
            out_ref[rows, :] = z
            hat, _ = norm(z, inner)
            h = hat * gain + bias
            mid_ref[rows, :] = (h * half_gelu(h)[2] * flags_ref[rows, 0:1]).astype(BF16)

    pipelined(product, rest, keep)


def fill_padded(padded_ref, source_ref):
    count, width = source_ref.shape
    padded_ref[0, 0:REACH, :] = jnp.zeros((REACH, width), BF16)
    padded_ref[0, count + REACH : count + 2 * REACH, :] = jnp.zeros((REACH, width), BF16)
    padded_ref[0, REACH : count + REACH, :] = source_ref[...]
    fill_further(padded_ref, count)


def fill_further(padded_ref, count):
    padded_ref[1, 0 : count + REACH, :] = padded_ref[0, DILATION : count + REACH + DILATION, :]


def shifted(padded_ref, flags, start, block, tap):
    which, at = tap % 2, start + tap // 2 * (2 * DILATION)
    if not isinstance(at, int):
        at = pl.multiple_of(at, 2 * DILATION)
    rows = padded_ref[which, pl.ds(at, block), :]
    if tap != KERNEL // 2:
        rows = rows * flags[:, tap + 1 : tap + 2]
    return rows


def conv_kernel(*refs):
    pieces, rest_refs = refs[: len(refs) - 22], refs[len(refs) - 22 :]
    (
        mid_hbm, down_ref, cot_ref, narrow_ref, now_flags_ref, place_ref,
        top_ref, low_ref, flat_hbm, sums_ref, wide_sums_ref,
        padded_ref, hold_ref, wide_weight_ref, weight_ref, flat_ref, taps_ref,
        out_ref, grad_ref, next_out_ref, next_grad_ref, semaphores,
    ) = rest_refs
    step = pl.program_id(0)
    block, width = out_ref.shape
    devices = hold_ref.shape[0]
    share = width // devices
    flat_copy = pltpu.make_async_copy(flat_ref, flat_hbm, semaphores.at[devices])

    @pl.when(step == 0)
    def _():
        count = mid_hbm.shape[0]
        copies = piece_copies(pieces, place_ref, hold_ref, semaphores)
        target = padded_ref.at[0, pl.ds(REACH, count)]
        mid_copy = pltpu.make_async_copy(mid_hbm, target, semaphores.at[devices + 1])
        mid_copy.start()
        for copy in copies:
            copy.start()
        padded_ref[0, 0:REACH, :] = jnp.zeros((REACH, width), BF16)
        padded_ref[0, count + REACH : count + 2 * REACH, :] = jnp.zeros((REACH, width), BF16)
        mid_copy.wait()
        fill_further(padded_ref, count)
        sums_ref[...] = jnp.zeros_like(sums_ref)
        wide_sums_ref[...] = jnp.zeros_like(wide_sums_ref)
        for copy in copies:
            copy.wait()
        for tap in range(KERNEL):
            for k in range(devices):
                item = hold_ref[k].astype(F32)
                wide_weight_ref[tap % 2, k * share : (k + 1) * share, :] = item[tap * share : (tap + 1) * share, :]
            part = wide_weight_ref[tap % 2].astype(BF16)
            weight_ref[tap * width : (tap + 1) * width, :] = part
            flat_ref[:, tap * width : (tap + 1) * width] = part
        flat_copy.start()

    def product():
        start = jnp.minimum(step, pl.num_programs(0) - 2) * block
        flags = now_flags_ref[...].astype(BF16)
        for tap in range(KERNEL):
            taps_ref[:, tap * width : (tap + 1) * width] = shifted(padded_ref, flags, start, block, tap)
        next_out_ref[...] = dot(taps_ref[...], weight_ref[...])
        next_grad_ref[...] = dot(cot_ref[...], down_ref[...])
        total = wide_sums_ref[...]
        for at in range(0, block, ROWS):
            total += fold(cot_ref[at : at + ROWS, :].astype(F32))
        wide_sums_ref[...] = total

    def keep():
        out_ref[...] = next_out_ref[...]
        grad_ref[...] = next_grad_ref[...]

    def rest():
        shift, gain, bias = narrow_ref[3:4, :], 0.5 * narrow_ref[4:5, :], 0.5 * narrow_ref[5:6, :]
        totals = [sums_ref[8 * k : 8 * k + 8, :] for k in range(3)]
        for at in range(0, block, ROWS):
            rows = slice(at, at + ROWS)
            hat, scale = norm(out_ref[rows, :] + shift, width)
            h = hat * gain + bias
            q, t, one_t = half_gelu(h)
            top_ref[rows, :] = (h * one_t).astype(BF16)
            slope2 = double_slope(h, q, t, one_t)
            back, by_gain, by_sum = back_parts(hat, scale, gain, slope2, grad_ref[rows, :], width)
            low_ref[rows, :] = back.astype(BF16)
            for k, part in enumerate((by_gain, by_sum, back)):
                totals[k] += fold(part)
        for k in range(3):
            sums_ref[8 * k : 8 * k + 8, :] = totals[k]

    pipelined(product, rest, keep)

    @pl.when(step == pl.num_programs(0) - 1)
    def _():
        flat_copy.wait()


def hand_out(place_ref, device, columns, ready_ref, rows, part):
    chip = device // 2
    m, n = (chip // columns) ^ place_ref[0], (chip % columns) ^ place_ref[1]
    which = (device % 2) ^ place_ref[2]
    if isinstance(rows, int):
        ready_ref[which, m, n, rows] = part.astype(ready_ref.dtype)
    else:
        ready_ref[which, m, n, rows, 0 : part.shape[1]] = part.astype(ready_ref.dtype)


def send_out(ready_ref, kept_hbm, sent_hbm, semaphores):
    copies = [
        pltpu.make_async_copy(ready_ref.at[k], target, semaphores.at[k])
        for k, target in enumerate((kept_hbm, sent_hbm))
    ]
    for copy in copies:
        copy.start()
    for copy in copies:
        copy.wait()


def weights_kernel(
    low_ref, mid_ref, flags_ref, place_ref, kept_hbm, sent_hbm,
    padded_ref, taps_ref, total_ref, row_ref, ready_ref, out_semaphores,
):
    count, width = mid_ref.shape
    columns = ready_ref.shape[2]
    devices = 2 * ready_ref.shape[1] * columns
    share = width // devices
    fill_padded(padded_ref, low_ref)
    flags = flags_ref[...].astype(BF16)
    for tap in range(KERNEL):
        taps_ref[:, tap * width : (tap + 1) * width] = shifted(padded_ref, flags, 0, count, KERNEL - 1 - tap)
    total_ref[...] = dot(mid_ref[...].T, taps_ref[...])
    row_ref[...] = jnp.zeros_like(row_ref)
    for device in range(devices):
        slot = device % row_ref.shape[0]
        for tap in range(KERNEL):
            part = total_ref[device * share : (device + 1) * share, tap * width : (tap + 1) * width]
            row_ref[slot, tap * share : (tap + 1) * share, :] = part
        hand_out(place_ref, device, columns, ready_ref, slice(None), row_ref[slot])
    send_out(ready_ref, kept_hbm, sent_hbm, out_semaphores)


def up_weight_kernel(
    act_ref, cot_ref, low_ref, top_ref, place_ref, kept_hbm, sent_hbm, total_ref, ready_ref, out_semaphores
):
    step, steps = pl.program_id(0), pl.num_programs(0)
    share = ready_ref.shape[4]
    devices = total_ref.shape[0] // share

    def part_of(group, left_ref, right_ref):
        total_ref[...] = dot(left_ref[...], right_ref[...], 0, 0)
        first = lax.rem(step, steps // 2) * devices
        for k in range(devices):
            part = total_ref[k * share : (k + 1) * share, :]
            hand_out(place_ref, first + k, ready_ref.shape[2], ready_ref, group, part)

    @pl.when(step < steps // 2)
    def _():
        part_of(0, act_ref, low_ref)

    @pl.when(step >= steps // 2)
    def _():
        part_of(1, cot_ref, top_ref)

    @pl.when(step == steps - 1)
    def _():
        send_out(ready_ref, kept_hbm, sent_hbm, out_semaphores)


def mid_grad_kernel(
    low_ref, flat_ref, up_out_ref, narrow_ref, now_flags_ref, flags_ref,
    up_low_ref, sums_ref,
    padded_ref, taps_ref, grad_ref, next_ref,
):
    step = pl.program_id(0)
    block, width = up_out_ref.shape

    @pl.when(step == 0)
    def _():
        fill_padded(padded_ref, low_ref)
        sums_ref[...] = jnp.zeros_like(sums_ref)

    def product():
        start = jnp.minimum(step, pl.num_programs(0) - 2) * block
        flags = now_flags_ref[...].astype(BF16)
        for tap in range(KERNEL):
            taps_ref[:, tap * width : (tap + 1) * width] = shifted(padded_ref, flags, start, block, KERNEL - 1 - tap)
        next_ref[...] = dot(taps_ref[...], flat_ref[...], 1, 1)

    def keep():
        grad_ref[...] = next_ref[...]

    def rest():
        gain, bias = 0.5 * narrow_ref[1:2, :], 0.5 * narrow_ref[2:3, :]
        totals = [sums_ref[8 * k : 8 * k + 8, :] for k in range(3)]
        for at in range(0, block, ROWS):
            rows = slice(at, at + ROWS)
            hat, scale = norm(up_out_ref[rows, :], width)
            h = hat * gain + bias
            slope2 = double_slope(h, *half_gelu(h))
            grad = grad_ref[rows, :] * flags_ref[rows, 0:1]
            back, by_gain, by_sum = back_parts(hat, scale, gain, slope2, grad, width)
            up_low_ref[rows, :] = back.astype(BF16)
            for k, part in enumerate((by_gain, by_sum, back)):
                totals[k] += fold(part)
        for k in range(3):
            sums_ref[8 * k : 8 * k + 8, :] = totals[k]

    pipelined(product, rest, keep)


def input_grad_kernel(
    up_low_ref, weight_ref, x_ref, cot_ref, wide_ref, top_sums_ref, mid_sums_ref, cot_sums_ref, place_ref,
    out_ref, kept_hbm, sent_hbm,
    grad_ref, next_ref, sums_ref, wide_row_ref, narrow_row_ref, ready_ref, out_semaphores,
):
    step, steps = pl.program_id(0), pl.num_programs(0)
    block, width = out_ref.shape

    @pl.when(step == 0)
    def _():
        sums_ref[...] = jnp.zeros_like(sums_ref)

    def product():
        next_ref[...] = dot(up_low_ref[...], weight_ref[...], 1, 1)

    def keep():
        grad_ref[...] = next_ref[...]

    def rest():
        gain, bias = 0.5 * wide_ref[0:1, :], 0.5 * wide_ref[1:2, :]
        by_gains, by_sums = sums_ref[0:8, :], sums_ref[8:16, :]
        for at in range(0, block, ROWS):
            rows = slice(at, at + ROWS)
            hat, scale = norm(x_ref[rows, :].astype(F32), width)
            h = hat * gain + bias
            slope2 = double_slope(h, *half_gelu(h))
            back, by_gain, by_sum = back_parts(hat, scale, gain, slope2, grad_ref[rows, :], width)
            out_ref[rows, :] = cot_ref[rows, :].astype(F32) + back
            by_gains += fold(by_gain)
            by_sums += fold(by_sum)
        sums_ref[0:8, :] = by_gains
        sums_ref[8:16, :] = by_sums

    pipelined(product, rest, keep)

    @pl.when(step == steps - 1)
    def _():
        def row(ref, k):
            return jnp.sum(ref[8 * k : 8 * k + 8, :], axis=0, keepdims=True)

        wide_row_ref[...] = jnp.zeros_like(wide_row_ref)
        narrow_row_ref[...] = jnp.zeros_like(narrow_row_ref)
        for at, (ref, k, factor) in enumerate(((sums_ref, 0, 0.5), (sums_ref, 1, 0.5), (cot_sums_ref, 0, 1.0))):
            wide_row_ref[at : at + 1, :] = factor * row(ref, k)
        rows = (
            (mid_sums_ref, 2, 1.0),
            (mid_sums_ref, 0, 0.5),
            (mid_sums_ref, 1, 0.5),
            (top_sums_ref, 2, 1.0),
            (top_sums_ref, 0, 0.5),
            (top_sums_ref, 1, 0.5),
        )
        for at, (ref, k, factor) in enumerate(rows):
            narrow_row_ref[at : at + 1, :] = factor * row(ref, k)
        columns = ready_ref.shape[2]
        devices = 2 * ready_ref.shape[1] * columns
        wide, narrow = width // devices, narrow_row_ref.shape[1] // devices
        ready_ref[...] = jnp.zeros_like(ready_ref)
        for device in range(devices):
            wide_part = wide_row_ref[:, device * wide : (device + 1) * wide]
            narrow_part = narrow_row_ref[:, device * narrow : (device + 1) * narrow]
            hand_out(place_ref, device, columns, ready_ref, slice(0, 8), wide_part)
            hand_out(place_ref, device, columns, ready_ref, slice(8, 16), narrow_part)
        send_out(ready_ref, kept_hbm, sent_hbm, out_semaphores)


def output_kernel(x_ref, top_ref, weight_ref, wide_ref, out_ref):
    product = dot(top_ref[...], weight_ref[...], 1, 1)
    out_ref[...] = (x_ref[...].astype(F32) + product + wide_ref[2:3, :]).astype(BF16)


def call(kernel, name, grid, ins, outs, scratch, flops, args):
    def spec(shape, rows):
        if rows in ("now", "past"):
            last = grid - 2
            place = (lambda i: jnp.minimum(i, last)) if rows == "now" else (lambda i: jnp.maximum(i - 1, 0))
            return pl.BlockSpec((shape[0] // (grid - 1),) + tuple(shape[1:]), lambda i: (place(i),) + (0,) * (len(shape) - 1))
        if rows == "any":
            return pl.BlockSpec(memory_space=pl.ANY)
        if rows == "smem":
            return pl.BlockSpec(memory_space=pltpu.SMEM)
        if rows in ("early half", "late half"):
            start = 0 if rows == "early half" else grid // 2
            return pl.BlockSpec((shape[0], shape[1] // 2), lambda i: (0, jnp.clip(i - start, 0, 1)))
        if rows is None:
            return pl.BlockSpec(shape, lambda i: (0,) * len(shape), pipeline_mode=pl.Buffered(1))
        return pl.BlockSpec((rows,) + tuple(shape[1:]), lambda i: (i,) + (0,) * (len(shape) - 1))

    results = [jax.ShapeDtypeStruct(shape, kind) for shape, kind, _ in outs]
    moved = sum(a.size * a.dtype.itemsize for a in list(args) + results) if flops > 1 else 1
    return pl.pallas_call(
        kernel,
        name=name,
        grid=(grid,),
        in_specs=[spec(a.shape, rows) for a, rows in zip(args, ins)],
        out_specs=[spec(shape, rows) for shape, _, rows in outs],
        out_shape=results,
        scratch_shapes=scratch,
        compiler_params=pltpu.CompilerParams(vmem_limit_bytes=VMEM_MIB[name] * 2**20),
        cost_estimate=pl.CostEstimate(flops=flops, bytes_accessed=moved, transcendentals=0),
    )(*args)


def flags_of(lengths_row, keep_mask):
    count = keep_mask.shape[0]
    ends = jnp.cumsum(lengths_row)
    position = jnp.arange(count, dtype=jnp.int32)[:, None]

    def segment(at):
        return jnp.sum((at >= ends[None, :]).astype(jnp.int32), axis=1, keepdims=True)

    own = segment(position)
    columns = [keep_mask[:, None] != 0]
    for tap in range(KERNEL):
        source = position + (tap - KERNEL // 2) * DILATION
        columns.append((source >= 0) & (source < count) & (segment(source) == own))
    columns += [columns[0]] * (8 - len(columns))
    return jnp.concatenate([column.astype(F32) for column in columns], axis=1)


def with_small(weight, wide, narrow):
    rows, width = weight.shape
    first = -(-rows // 8) * 8
    out = jnp.pad(weight, ((0, first + 8 - rows), (0, 0)))
    for lane, group in ((0, wide), (128, narrow)):
        for k, item in enumerate(group):
            after = width - lane - item.shape[0]
            out = out + jnp.pad(item[None, :], ((first + k, 7 - k), (lane, after)))
    return out


def padded_rows(rows):
    return -(-rows // 8) * 8


def body(
    axes,
    inputs,
    lengths,
    keep_mask,
    cotangent,
    ln1_gain,
    ln1_bias,
    up_weight,
    up_bias,
    ln2_gain,
    ln2_bias,
    conv_weight,
    conv_bias,
    ln3_gain,
    ln3_bias,
    down_weight,
    down_bias,
):
    count, model = inputs.shape
    inner = up_weight.shape[1]
    dp, columns = axes[0][1], axes[1][1]
    chips = dp * columns
    place = jnp.stack([lax.axis_index(name) for name, _ in axes]).astype(jnp.int32)
    flags = flags_of(lengths[0], keep_mask)
    share, conv_share = model // (2 * chips), KERNEL * inner // (2 * chips)

    conv_rows = padded_rows(conv_share)
    up_block = with_small(
        jnp.concatenate([up_weight, down_weight.T]),
        (ln1_gain, ln1_bias, down_bias),
        (up_bias, ln2_gain, ln2_bias, conv_bias, ln3_gain, ln3_bias),
    )
    conv_block = jnp.pad(conv_weight.reshape(-1, inner), ((0, conv_rows - conv_share), (0, 0)))
    up_one = jnp.stack(gather_stage(up_block, axes[1]))
    up_two = gather_stage(up_one, axes[0])
    name, size = axes[1]
    late_block = after(conv_block, up_one)
    conv_near = [conv_block, swap(conv_block, name, size, 1)]
    conv_near += [swap(late_block, name, size, mask) for mask in range(2, size)]
    conv_one = jnp.stack(after(tuple(conv_near), *up_two))
    conv_two = gather_stage(conv_one, axes[0])
    up_pieces = core_stage([jnp.stack(after(tuple(up_two), *conv_near))], axes)

    block, large = 256, 512
    steps = count // block
    wide_up = 2 * count * model * inner
    wide_conv = 2 * count * KERNEL * inner * inner
    padded = pltpu.VMEM((2, count + 2 * REACH, inner), BF16)

    act_one, up_full, down_full, wide, narrow, up_out, mid = call(
        up_kernel, "up", steps + 1, ("any", "any", "now", "past", "smem"),
        [
            ((count, model), BF16, "now"),
            ((model, inner), BF16, None),
            ((model, inner), BF16, None),
            ((8, model), F32, None),
            ((8, inner), F32, None),
            ((count, inner), F32, "past"),
            ((count, inner), BF16, "past"),
        ],
        [
            pltpu.VMEM((2 * chips,) + up_block.shape, BF16),
            pltpu.VMEM((model, inner), F32),
            pltpu.VMEM((model, inner), F32),
            pltpu.VMEM((block, inner), F32),
            pltpu.VMEM((block, inner), F32),
            pltpu.SemaphoreType.DMA((2 * chips,)),
        ],
        wide_up, (*up_pieces, inputs, flags, after(place, conv_one)),
    )
    conv_pieces = core_stage(conv_two[:1] + list(after(tuple(conv_two[1:]), mid)), axes)
    top, low, conv_flat, top_sums, cot_sums = call(
        conv_kernel, "conv", steps + 1, ("any",) * len(conv_pieces) + ("any", None, "now", None, "now", "smem"),
        [
            ((count, inner), BF16, "past"),
            ((count, inner), BF16, "past"),
            ((inner, KERNEL * inner), BF16, "any"),
            ((24, inner), F32, None),
            ((8, model), F32, None),
        ],
        [
            padded,
            pltpu.VMEM((2 * chips,) + conv_block.shape, BF16),
            pltpu.VMEM((2, inner, inner), F32),
            pltpu.VMEM((KERNEL * inner, inner), BF16),
            pltpu.VMEM((inner, KERNEL * inner), BF16),
            pltpu.VMEM((block, KERNEL * inner), BF16),
        ]
        + [pltpu.VMEM((block, inner), F32)] * 4
        + [pltpu.SemaphoreType.DMA((2 * chips + 2,))],
        wide_conv + wide_up, (*conv_pieces, mid, down_full, cotangent, narrow, flags, place),
    )
    conv_kept, conv_sent = call(
        weights_kernel, "weights", 1, (None, None, None, "smem"),
        [((dp, columns, conv_rows, inner), BF16, "any")] * 2,
        [
            padded,
            pltpu.VMEM((count, KERNEL * inner), BF16),
            pltpu.VMEM((inner, KERNEL * inner), F32),
            pltpu.VMEM((4, conv_rows, inner), F32),
            pltpu.VMEM((2, dp, columns, conv_rows, inner), BF16),
            pltpu.SemaphoreType.DMA((2,)),
        ],
        wide_conv, (low, mid, flags, place),
    )
    (output,) = call(
        output_kernel, "output", count // large, (large, large, None, None),
        [((count, model), BF16, large)],
        [], wide_up, (inputs, top, down_full, after(wide, conv_sent)),
    )
    conv_grad = add_up(after(conv_kept, output), [swap(conv_sent, *axes[2], 1)])
    conv_stage = scatter_stage(conv_grad, axes[0])
    up_low, mid_sums = call(
        mid_grad_kernel, "mid_grad", steps + 1, (None, None, "past", None, "now", "past"),
        [((count, inner), BF16, "past"), ((24, inner), F32, None)],
        [
            padded,
            pltpu.VMEM((block, KERNEL * inner), BF16),
            pltpu.VMEM((block, inner), F32),
            pltpu.VMEM((block, inner), F32),
        ],
        wide_conv, (low, conv_flat, up_out, after(narrow, conv_grad), flags, flags),
    )
    up_kept, up_sent = call(
        up_weight_kernel, "up_weight", 4, ("early half", "late half", None, None, "smem"),
        [((dp, columns, 2, share, inner), BF16, "any")] * 2,
        [
            pltpu.VMEM((model // 2, inner), F32),
            pltpu.VMEM((2, dp, columns, 2, share, inner), BF16),
            pltpu.SemaphoreType.DMA((2,)),
        ],
        1, (act_one, cotangent, up_low, top, place),
    )
    conv_arrived = after(tuple(conv_stage[1]), up_kept)
    up_grad = add_up(up_kept, [swap(after(up_sent, *conv_arrived), *axes[2], 1)])
    up_stage = scatter_stage(up_grad, axes[0])
    conv_grad = add_up(conv_stage[0], conv_arrived)
    conv_stage = scatter_stage(conv_grad, axes[1])
    input_grad, small_kept, small_sent = call(
        input_grad_kernel, "input_grad", steps + 1,
        ("now", None, "past", "past", None, None, None, None, "smem"),
        [((count, model), F32, "past")] + [((dp, columns, 16, 128), F32, "any")] * 2,
        [
            pltpu.VMEM((block, model), F32),
            pltpu.VMEM((block, model), F32),
            pltpu.VMEM((16, model), F32),
            pltpu.VMEM((8, model), F32),
            pltpu.VMEM((8, inner), F32),
            pltpu.VMEM((2, dp, columns, 16, 128), F32),
            pltpu.SemaphoreType.DMA((2,)),
        ],
        wide_up,
        (up_low, up_full, inputs, cotangent, wide, top_sums, mid_sums, cot_sums, after(place, conv_grad, up_grad)),
    )
    up_arrived, conv_arrived = after((tuple(up_stage[1]), tuple(conv_stage[1])), small_kept)
    small = small_kept + swap(after(small_sent, *up_arrived, *conv_arrived), *axes[2], 1)
    up_stage = scatter_stage(add_up(up_stage[0], up_arrived), axes[1])
    small_own = exact_stage(exact_stage(small, axes[0]), axes[1])
    conv_own = add_up(conv_stage[0], conv_arrived)[0:conv_share]
    up_own, down_own = add_up(*up_stage)
    wide_row, narrow_row = up_weight.shape[0], conv_weight.shape[1]
    sums = [small_own[at, :wide_row] for at in range(2)]
    sums += [small_own[8 + at, :narrow_row] for at in range(6)]
    sums.append(small_own[2, :wide_row])
    return (output, input_grad, up_own, conv_own.reshape(conv_weight.shape), down_own.T) + tuple(sums)


def solution(mesh):
    rows, columns = mesh.shape["dp"], mesh.shape["fsdp"] // 2
    split = Mesh(mesh.devices.reshape(rows, columns, 2), ALL)
    axes = (("dp", rows), ("chip", columns), ("core", 2))
    by_row = P(ALL)
    by_second = P(None, ALL)
    in_specs = [by_row] * 16
    in_specs[10] = in_specs[14] = by_second
    out_specs = [by_row] * 14
    out_specs[3] = out_specs[4] = by_second
    return jax.shard_map(
        functools.partial(body, axes),
        mesh=split,
        in_specs=tuple(in_specs),
        out_specs=tuple(out_specs),
        check_vma=False,
    )
```

```python
import functools

import jax
import jax.numpy as jnp
from jax import lax
from jax.experimental import pallas as pl
from jax.experimental.pallas import tpu as pltpu
from jax.sharding import Mesh
from jax.sharding import PartitionSpec as P

KERNEL = 5
DILATION = 8
REACH = KERNEL // 2 * DILATION
ALL = ("dp", "chip", "core")
F32 = jnp.float32
BF16 = jnp.bfloat16
TANH_ONE = 0.7978845608028654
TANH_THREE = TANH_ONE * 0.044715
ROWS = 32
VMEM_MIB = {"first_act": 61, "up": 61, "conv": 61, "weights": 44, "mid_grad": 24, "up_weight": 30, "input_grad": 20, "output": 12}


def swap(array, axis, size, mask):
    return lax.ppermute(array, axis, [(k, k ^ mask) for k in range(size)])


def after(value, *others):
    return lax.optimization_barrier((value, *others))[0]


def gather_stage(block, axis):
    name, size = axis
    return [block] + [swap(block, name, size, mask) for mask in range(1, size)]


def core_stage(pieces, axes):
    return pieces + [swap(piece, axes[2][0], axes[2][1], 1) for piece in pieces]


def scatter_stage(total, axis):
    name, size = axis
    arrived = [swap(total[mask].astype(BF16), name, size, mask) for mask in range(1, size)]
    return total[0], arrived


def add_up(kept, arrived):
    total = kept.astype(F32)
    for item in arrived:
        total = total + item.astype(F32)
    return total


def exact_stage(total, axis):
    name, size = axis
    return total[0] + sum(swap(total[mask], name, size, mask) for mask in range(1, size))


def norm(z, width):
    center = z - jnp.sum(z, axis=1, keepdims=True) * (1.0 / width)
    scale = lax.rsqrt(jnp.sum(center * center, axis=1, keepdims=True) * (1.0 / width) + 1e-05)
    return center * scale, scale


def pipelined(product, rest, keep):
    step, last = pl.program_id(0), pl.num_programs(0) - 1

    @pl.when(step == 0)
    def _():
        product()
        keep()

    @pl.when((step > 0) & (step < last))
    def _():
        product()
        rest()
        keep()

    @pl.when(step == last)
    def _():
        rest()


def half_gelu(h):
    q = h * h
    t = jnp.tanh(h * (2.0 * TANH_ONE + 8.0 * TANH_THREE * q))
    return q, t, 1.0 + t


def double_slope(h, q, t, one_t):
    return one_t * (1.0 + (1.0 - t) * (h * (2.0 * TANH_ONE + 24.0 * TANH_THREE * q)))


def back_parts(hat, scale, half_gain, slope2, grad, width):
    by_sum = slope2 * grad
    by_gain = by_sum * hat
    by_hat = by_sum * half_gain
    first = jnp.sum(by_hat, axis=1, keepdims=True) * (scale * (1.0 / width))
    second = jnp.sum(by_hat * hat, axis=1, keepdims=True) * (scale * (1.0 / width))
    return scale * by_hat - first - hat * second, by_gain, by_sum


def fold(value):
    return sum(value[k : k + 8] for k in range(0, value.shape[0], 8))


def dot(left, right, left_dim=1, right_dim=0):
    return lax.dot_general(
        left, right, (((left_dim,), (right_dim,)), ((), ())), preferred_element_type=F32
    )


def piece_copies(pieces, place_ref, hold_ref, semaphores):
    half = len(pieces) // 2
    columns = pieces[0].shape[0]
    copies = []
    for c in range(2):
        for o in range(half):
            for i in range(columns):
                chip = (place_ref[0] ^ o) * columns + (place_ref[1] ^ i)
                target = hold_ref.at[2 * chip + (place_ref[2] ^ c)]
                copies.append(pltpu.make_async_copy(pieces[c * half + o].at[i], target, semaphores.at[len(copies)]))
    return copies


def up_kernel(*refs):
    pieces, rest_refs = refs[: len(refs) - 16], refs[len(refs) - 16 :]
    (
        x_ref, flags_ref, place_ref,
        act_ref, up_ref, down_ref, wide_ref, narrow_ref, out_ref, mid_ref,
        hold_ref, up_wide_ref, down_wide_ref, z_ref, next_ref, semaphores,
    ) = rest_refs
    block, width = x_ref.shape
    inner = z_ref.shape[1]

    @pl.when(pl.program_id(0) == 0)
    def _():
        copies = piece_copies(pieces, place_ref, hold_ref, semaphores)
        for copy in copies:
            copy.start()
        for copy in copies:
            copy.wait()
        devices = hold_ref.shape[0]
        share, of_narrow = width // devices, narrow_ref.shape[1] // devices
        for k in range(devices):
            item = hold_ref[k].astype(F32)
            small = item[item.shape[0] - 8 :, :]
            wide_ref[:, k * share : (k + 1) * share] = small[:, 0:share]
            narrow_ref[:, k * of_narrow : (k + 1) * of_narrow] = small[:, 128 : 128 + of_narrow]
            up_wide_ref[k * share : (k + 1) * share, :] = item[0:share, :]
            down_wide_ref[k * share : (k + 1) * share, :] = item[share : 2 * share, :]
        up_ref[...] = up_wide_ref[...].astype(BF16)
        down_ref[...] = down_wide_ref[...].astype(BF16)

    def product():
        gain, bias = 0.5 * wide_ref[0:1, :], 0.5 * wide_ref[1:2, :]
        for at in range(0, block, ROWS):
            rows = slice(at, at + ROWS)
            hat, _ = norm(x_ref[rows, :].astype(F32), width)
            h = hat * gain + bias
            act_ref[rows, :] = (h * half_gelu(h)[2]).astype(BF16)
        next_ref[...] = dot(act_ref[...], up_ref[...])

    def keep():
        z_ref[...] = next_ref[...]

    def rest():
        shift, gain, bias = narrow_ref[0:1, :], 0.5 * narrow_ref[1:2, :], 0.5 * narrow_ref[2:3, :]
        for at in range(0, block, ROWS):
            rows = slice(at, at + ROWS)
            z = z_ref[rows, :] + shift
            out_ref[rows, :] = z
            hat, _ = norm(z, inner)
            h = hat * gain + bias
            mid_ref[rows, :] = (h * half_gelu(h)[2] * flags_ref[rows, 0:1]).astype(BF16)

    pipelined(product, rest, keep)


def fill_padded(padded_ref, source_ref):
    count, width = source_ref.shape
    padded_ref[0, 0:REACH, :] = jnp.zeros((REACH, width), BF16)
    padded_ref[0, count + REACH : count + 2 * REACH, :] = jnp.zeros((REACH, width), BF16)
    padded_ref[0, REACH : count + REACH, :] = source_ref[...]
    fill_further(padded_ref, count)


def fill_further(padded_ref, count):
    padded_ref[1, 0 : count + REACH, :] = padded_ref[0, DILATION : count + REACH + DILATION, :]


def shifted(padded_ref, flags, start, block, tap):
    which, at = tap % 2, start + tap // 2 * (2 * DILATION)
    if not isinstance(at, int):
        at = pl.multiple_of(at, 2 * DILATION)
    rows = padded_ref[which, pl.ds(at, block), :]
    if tap != KERNEL // 2:
        rows = rows * flags[:, tap + 1 : tap + 2]
    return rows


def conv_kernel(*refs):
    pieces, rest_refs = refs[: len(refs) - 22], refs[len(refs) - 22 :]
    (
        mid_hbm, down_ref, cot_ref, narrow_ref, now_flags_ref, place_ref,
        top_ref, low_ref, flat_hbm, sums_ref, wide_sums_ref,
        padded_ref, hold_ref, wide_weight_ref, weight_ref, flat_ref, taps_ref,
        out_ref, grad_ref, next_out_ref, next_grad_ref, semaphores,
    ) = rest_refs
    step = pl.program_id(0)
    block, width = out_ref.shape
    devices = hold_ref.shape[0]
    share = width // devices
    flat_copy = pltpu.make_async_copy(flat_ref, flat_hbm, semaphores.at[devices])

    @pl.when(step == 0)
    def _():
        count = mid_hbm.shape[0]
        copies = piece_copies(pieces, place_ref, hold_ref, semaphores)
        target = padded_ref.at[0, pl.ds(REACH, count)]
        mid_copy = pltpu.make_async_copy(mid_hbm, target, semaphores.at[devices + 1])
        mid_copy.start()
        for copy in copies:
            copy.start()
        padded_ref[0, 0:REACH, :] = jnp.zeros((REACH, width), BF16)
        padded_ref[0, count + REACH : count + 2 * REACH, :] = jnp.zeros((REACH, width), BF16)
        mid_copy.wait()
        fill_further(padded_ref, count)
        sums_ref[...] = jnp.zeros_like(sums_ref)
        wide_sums_ref[...] = jnp.zeros_like(wide_sums_ref)
        for copy in copies:
            copy.wait()
        for tap in range(KERNEL):
            for k in range(devices):
                item = hold_ref[k].astype(F32)
                wide_weight_ref[tap % 2, k * share : (k + 1) * share, :] = item[tap * share : (tap + 1) * share, :]
            part = wide_weight_ref[tap % 2].astype(BF16)
            weight_ref[tap * width : (tap + 1) * width, :] = part
            flat_ref[:, tap * width : (tap + 1) * width] = part
        flat_copy.start()

    def product():
        start = jnp.minimum(step, pl.num_programs(0) - 2) * block
        flags = now_flags_ref[...].astype(BF16)
        for tap in range(KERNEL):
            taps_ref[:, tap * width : (tap + 1) * width] = shifted(padded_ref, flags, start, block, tap)
        next_out_ref[...] = dot(taps_ref[...], weight_ref[...])
        next_grad_ref[...] = dot(cot_ref[...], down_ref[...])
        total = wide_sums_ref[...]
        for at in range(0, block, ROWS):
            total += fold(cot_ref[at : at + ROWS, :].astype(F32))
        wide_sums_ref[...] = total

    def keep():
        out_ref[...] = next_out_ref[...]
        grad_ref[...] = next_grad_ref[...]

    def rest():
        shift, gain, bias = narrow_ref[3:4, :], 0.5 * narrow_ref[4:5, :], 0.5 * narrow_ref[5:6, :]
        totals = [sums_ref[8 * k : 8 * k + 8, :] for k in range(3)]
        for at in range(0, block, ROWS):
            rows = slice(at, at + ROWS)
            hat, scale = norm(out_ref[rows, :] + shift, width)
            h = hat * gain + bias
            q, t, one_t = half_gelu(h)
            top_ref[rows, :] = (h * one_t).astype(BF16)
            slope2 = double_slope(h, q, t, one_t)
            back, by_gain, by_sum = back_parts(hat, scale, gain, slope2, grad_ref[rows, :], width)
            low_ref[rows, :] = back.astype(BF16)
            for k, part in enumerate((by_gain, by_sum, back)):
                totals[k] += fold(part)
        for k in range(3):
            sums_ref[8 * k : 8 * k + 8, :] = totals[k]

    pipelined(product, rest, keep)

    @pl.when(step == pl.num_programs(0) - 1)
    def _():
        flat_copy.wait()


def hand_out(place_ref, device, columns, ready_ref, rows, part):
    chip = device // 2
    m, n = (chip // columns) ^ place_ref[0], (chip % columns) ^ place_ref[1]
    which = (device % 2) ^ place_ref[2]
    if isinstance(rows, int):
        ready_ref[which, m, n, rows] = part.astype(ready_ref.dtype)
    else:
        ready_ref[which, m, n, rows, 0 : part.shape[1]] = part.astype(ready_ref.dtype)


def send_out(ready_ref, kept_hbm, sent_hbm, semaphores):
    copies = [
        pltpu.make_async_copy(ready_ref.at[k], target, semaphores.at[k])
        for k, target in enumerate((kept_hbm, sent_hbm))
    ]
    for copy in copies:
        copy.start()
    for copy in copies:
        copy.wait()


def weights_kernel(
    low_ref, mid_ref, flags_ref, place_ref, kept_hbm, sent_hbm,
    padded_ref, taps_ref, total_ref, row_ref, ready_ref, out_semaphores,
):
    count, width = mid_ref.shape
    columns = ready_ref.shape[2]
    devices = 2 * ready_ref.shape[1] * columns
    share = width // devices
    fill_padded(padded_ref, low_ref)
    flags = flags_ref[...].astype(BF16)
    for tap in range(KERNEL):
        taps_ref[:, tap * width : (tap + 1) * width] = shifted(padded_ref, flags, 0, count, KERNEL - 1 - tap)
    total_ref[...] = dot(mid_ref[...].T, taps_ref[...])
    row_ref[...] = jnp.zeros_like(row_ref)
    for device in range(devices):
        slot = device % row_ref.shape[0]
        for tap in range(KERNEL):
            part = total_ref[device * share : (device + 1) * share, tap * width : (tap + 1) * width]
            row_ref[slot, tap * share : (tap + 1) * share, :] = part
        hand_out(place_ref, device, columns, ready_ref, slice(None), row_ref[slot])
    send_out(ready_ref, kept_hbm, sent_hbm, out_semaphores)


def up_weight_kernel(
    act_ref, cot_ref, low_ref, top_ref, place_ref, kept_hbm, sent_hbm, total_ref, ready_ref, out_semaphores
):
    step, steps = pl.program_id(0), pl.num_programs(0)
    share = ready_ref.shape[4]
    devices = total_ref.shape[0] // share

    def part_of(group, left_ref, right_ref):
        total_ref[...] = dot(left_ref[...], right_ref[...], 0, 0)
        first = lax.rem(step, steps // 2) * devices
        for k in range(devices):
            part = total_ref[k * share : (k + 1) * share, :]
            hand_out(place_ref, first + k, ready_ref.shape[2], ready_ref, group, part)

    @pl.when(step < steps // 2)
    def _():
        part_of(0, act_ref, low_ref)

    @pl.when(step >= steps // 2)
    def _():
        part_of(1, cot_ref, top_ref)

    @pl.when(step == steps - 1)
    def _():
        send_out(ready_ref, kept_hbm, sent_hbm, out_semaphores)


def mid_grad_kernel(
    low_ref, flat_ref, up_out_ref, narrow_ref, now_flags_ref, flags_ref,
    up_low_ref, sums_ref,
    padded_ref, taps_ref, grad_ref, next_ref,
):
    step = pl.program_id(0)
    block, width = up_out_ref.shape

    @pl.when(step == 0)
    def _():
        fill_padded(padded_ref, low_ref)
        sums_ref[...] = jnp.zeros_like(sums_ref)

    def product():
        start = jnp.minimum(step, pl.num_programs(0) - 2) * block
        flags = now_flags_ref[...].astype(BF16)
        for tap in range(KERNEL):
            taps_ref[:, tap * width : (tap + 1) * width] = shifted(padded_ref, flags, start, block, KERNEL - 1 - tap)
        next_ref[...] = dot(taps_ref[...], flat_ref[...], 1, 1)

    def keep():
        grad_ref[...] = next_ref[...]

    def rest():
        gain, bias = 0.5 * narrow_ref[1:2, :], 0.5 * narrow_ref[2:3, :]
        totals = [sums_ref[8 * k : 8 * k + 8, :] for k in range(3)]
        for at in range(0, block, ROWS):
            rows = slice(at, at + ROWS)
            hat, scale = norm(up_out_ref[rows, :], width)
            h = hat * gain + bias
            slope2 = double_slope(h, *half_gelu(h))
            grad = grad_ref[rows, :] * flags_ref[rows, 0:1]
            back, by_gain, by_sum = back_parts(hat, scale, gain, slope2, grad, width)
            up_low_ref[rows, :] = back.astype(BF16)
            for k, part in enumerate((by_gain, by_sum, back)):
                totals[k] += fold(part)
        for k in range(3):
            sums_ref[8 * k : 8 * k + 8, :] = totals[k]

    pipelined(product, rest, keep)


def input_grad_kernel(
    up_low_ref, weight_ref, x_ref, cot_ref, wide_ref, top_sums_ref, mid_sums_ref, cot_sums_ref, place_ref,
    out_ref, kept_hbm, sent_hbm,
    grad_ref, next_ref, sums_ref, wide_row_ref, narrow_row_ref, ready_ref, out_semaphores,
):
    step, steps = pl.program_id(0), pl.num_programs(0)
    block, width = out_ref.shape

    @pl.when(step == 0)
    def _():
        sums_ref[...] = jnp.zeros_like(sums_ref)

    def product():
        next_ref[...] = dot(up_low_ref[...], weight_ref[...], 1, 1)

    def keep():
        grad_ref[...] = next_ref[...]

    def rest():
        gain, bias = 0.5 * wide_ref[0:1, :], 0.5 * wide_ref[1:2, :]
        by_gains, by_sums = sums_ref[0:8, :], sums_ref[8:16, :]
        for at in range(0, block, ROWS):
            rows = slice(at, at + ROWS)
            hat, scale = norm(x_ref[rows, :].astype(F32), width)
            h = hat * gain + bias
            slope2 = double_slope(h, *half_gelu(h))
            back, by_gain, by_sum = back_parts(hat, scale, gain, slope2, grad_ref[rows, :], width)
            out_ref[rows, :] = cot_ref[rows, :].astype(F32) + back
            by_gains += fold(by_gain)
            by_sums += fold(by_sum)
        sums_ref[0:8, :] = by_gains
        sums_ref[8:16, :] = by_sums

    pipelined(product, rest, keep)

    @pl.when(step == steps - 1)
    def _():
        def row(ref, k):
            return jnp.sum(ref[8 * k : 8 * k + 8, :], axis=0, keepdims=True)

        wide_row_ref[...] = jnp.zeros_like(wide_row_ref)
        narrow_row_ref[...] = jnp.zeros_like(narrow_row_ref)
        for at, (ref, k, factor) in enumerate(((sums_ref, 0, 0.5), (sums_ref, 1, 0.5), (cot_sums_ref, 0, 1.0))):
            wide_row_ref[at : at + 1, :] = factor * row(ref, k)
        rows = (
            (mid_sums_ref, 2, 1.0),
            (mid_sums_ref, 0, 0.5),
            (mid_sums_ref, 1, 0.5),
            (top_sums_ref, 2, 1.0),
            (top_sums_ref, 0, 0.5),
            (top_sums_ref, 1, 0.5),
        )
        for at, (ref, k, factor) in enumerate(rows):
            narrow_row_ref[at : at + 1, :] = factor * row(ref, k)
        columns = ready_ref.shape[2]
        devices = 2 * ready_ref.shape[1] * columns
        wide, narrow = width // devices, narrow_row_ref.shape[1] // devices
        ready_ref[...] = jnp.zeros_like(ready_ref)
        for device in range(devices):
            wide_part = wide_row_ref[:, device * wide : (device + 1) * wide]
            narrow_part = narrow_row_ref[:, device * narrow : (device + 1) * narrow]
            hand_out(place_ref, device, columns, ready_ref, slice(0, 8), wide_part)
            hand_out(place_ref, device, columns, ready_ref, slice(8, 16), narrow_part)
        send_out(ready_ref, kept_hbm, sent_hbm, out_semaphores)


def output_kernel(x_ref, top_ref, weight_ref, wide_ref, out_ref):
    product = dot(top_ref[...], weight_ref[...], 1, 1)
    out_ref[...] = (x_ref[...].astype(F32) + product + wide_ref[2:3, :]).astype(BF16)


def call(kernel, name, grid, ins, outs, scratch, flops, args):
    def spec(shape, rows):
        if rows in ("now", "past"):
            last = grid - 2
            place = (lambda i: jnp.minimum(i, last)) if rows == "now" else (lambda i: jnp.maximum(i - 1, 0))
            return pl.BlockSpec((shape[0] // (grid - 1),) + tuple(shape[1:]), lambda i: (place(i),) + (0,) * (len(shape) - 1))
        if rows == "any":
            return pl.BlockSpec(memory_space=pl.ANY)
        if rows == "smem":
            return pl.BlockSpec(memory_space=pltpu.SMEM)
        if rows in ("early half", "late half"):
            start = 0 if rows == "early half" else grid // 2
            return pl.BlockSpec((shape[0], shape[1] // 2), lambda i: (0, jnp.clip(i - start, 0, 1)))
        if rows is None:
            return pl.BlockSpec(shape, lambda i: (0,) * len(shape), pipeline_mode=pl.Buffered(1))
        return pl.BlockSpec((rows,) + tuple(shape[1:]), lambda i: (i,) + (0,) * (len(shape) - 1))

    results = [jax.ShapeDtypeStruct(shape, kind) for shape, kind, _ in outs]
    moved = sum(a.size * a.dtype.itemsize for a in list(args) + results) if flops > 1 else 1
    return pl.pallas_call(
        kernel,
        name=name,
        grid=(grid,),
        in_specs=[spec(a.shape, rows) for a, rows in zip(args, ins)],
        out_specs=[spec(shape, rows) for shape, _, rows in outs],
        out_shape=results,
        scratch_shapes=scratch,
        compiler_params=pltpu.CompilerParams(vmem_limit_bytes=VMEM_MIB[name] * 2**20),
        cost_estimate=pl.CostEstimate(flops=flops, bytes_accessed=moved, transcendentals=0),
    )(*args)


def flags_of(lengths_row, keep_mask):
    count = keep_mask.shape[0]
    ends = jnp.cumsum(lengths_row)
    position = jnp.arange(count, dtype=jnp.int32)[:, None]

    def segment(at):
        return jnp.sum((at >= ends[None, :]).astype(jnp.int32), axis=1, keepdims=True)

    own = segment(position)
    columns = [keep_mask[:, None] != 0]
    for tap in range(KERNEL):
        source = position + (tap - KERNEL // 2) * DILATION
        columns.append((source >= 0) & (source < count) & (segment(source) == own))
    columns += [columns[0]] * (8 - len(columns))
    return jnp.concatenate([column.astype(F32) for column in columns], axis=1)


def with_small(weight, wide, narrow):
    rows, width = weight.shape
    first = -(-rows // 8) * 8
    out = jnp.pad(weight, ((0, first + 8 - rows), (0, 0)))
    for lane, group in ((0, wide), (128, narrow)):
        for k, item in enumerate(group):
            after = width - lane - item.shape[0]
            out = out + jnp.pad(item[None, :], ((first + k, 7 - k), (lane, after)))
    return out


def padded_rows(rows):
    return -(-rows // 8) * 8


def body(
    axes,
    inputs,
    lengths,
    keep_mask,
    cotangent,
    ln1_gain,
    ln1_bias,
    up_weight,
    up_bias,
    ln2_gain,
    ln2_bias,
    conv_weight,
    conv_bias,
    ln3_gain,
    ln3_bias,
    down_weight,
    down_bias,
):
    count, model = inputs.shape
    inner = up_weight.shape[1]
    dp, columns = axes[0][1], axes[1][1]
    chips = dp * columns
    place = jnp.stack([lax.axis_index(name) for name, _ in axes]).astype(jnp.int32)
    flags = flags_of(lengths[0], keep_mask)
    share, conv_share = model // (2 * chips), KERNEL * inner // (2 * chips)

    conv_rows = padded_rows(conv_share)
    up_block = with_small(
        jnp.concatenate([up_weight, down_weight.T]),
        (ln1_gain, ln1_bias, down_bias),
        (up_bias, ln2_gain, ln2_bias, conv_bias, ln3_gain, ln3_bias),
    )
    conv_block = jnp.pad(conv_weight.reshape(-1, inner), ((0, conv_rows - conv_share), (0, 0)))
    up_one = jnp.stack(gather_stage(up_block, axes[1]))
    up_two = gather_stage(up_one, axes[0])
    name, size = axes[1]
    late_block = after(conv_block, up_one)
    conv_near = [conv_block, swap(conv_block, name, size, 1)]
    conv_near += [swap(late_block, name, size, mask) for mask in range(2, size)]
    conv_one = jnp.stack(after(tuple(conv_near), *up_two))
    conv_two = gather_stage(conv_one, axes[0])
    up_pieces = core_stage(up_two[:1] + list(after(tuple(up_two[1:]), *conv_near)), axes)

    block, large = 256, 512
    steps = count // block
    wide_up = 2 * count * model * inner
    wide_conv = 2 * count * KERNEL * inner * inner
    padded = pltpu.VMEM((2, count + 2 * REACH, inner), BF16)

    act_one, up_full, down_full, wide, narrow, up_out, mid = call(
        up_kernel, "up", steps + 1, ("any",) * len(up_pieces) + ("now", "past", "smem"),
        [
            ((count, model), BF16, "now"),
            ((model, inner), BF16, None),
            ((model, inner), BF16, None),
            ((8, model), F32, None),
            ((8, inner), F32, None),
            ((count, inner), F32, "past"),
            ((count, inner), BF16, "past"),
        ],
        [
            pltpu.VMEM((2 * chips,) + up_block.shape, BF16),
            pltpu.VMEM((model, inner), F32),
            pltpu.VMEM((model, inner), F32),
            pltpu.VMEM((block, inner), F32),
            pltpu.VMEM((block, inner), F32),
            pltpu.SemaphoreType.DMA((2 * chips,)),
        ],
        wide_up, (*up_pieces, inputs, flags, after(place, conv_one)),
    )
    conv_pieces = core_stage(conv_two[:1] + list(after(tuple(conv_two[1:]), mid)), axes)
    top, low, conv_flat, top_sums, cot_sums = call(
        conv_kernel, "conv", steps + 1, ("any",) * len(conv_pieces) + ("any", None, "now", None, "now", "smem"),
        [
            ((count, inner), BF16, "past"),
            ((count, inner), BF16, "past"),
            ((inner, KERNEL * inner), BF16, "any"),
            ((24, inner), F32, None),
            ((8, model), F32, None),
        ],
        [
            padded,
            pltpu.VMEM((2 * chips,) + conv_block.shape, BF16),
            pltpu.VMEM((2, inner, inner), F32),
            pltpu.VMEM((KERNEL * inner, inner), BF16),
            pltpu.VMEM((inner, KERNEL * inner), BF16),
            pltpu.VMEM((block, KERNEL * inner), BF16),
        ]
        + [pltpu.VMEM((block, inner), F32)] * 4
        + [pltpu.SemaphoreType.DMA((2 * chips + 2,))],
        wide_conv + wide_up, (*conv_pieces, mid, down_full, cotangent, narrow, flags, place),
    )
    conv_kept, conv_sent = call(
        weights_kernel, "weights", 1, (None, None, None, "smem"),
        [((dp, columns, conv_rows, inner), BF16, "any")] * 2,
        [
            padded,
            pltpu.VMEM((count, KERNEL * inner), BF16),
            pltpu.VMEM((inner, KERNEL * inner), F32),
            pltpu.VMEM((4, conv_rows, inner), F32),
            pltpu.VMEM((2, dp, columns, conv_rows, inner), BF16),
            pltpu.SemaphoreType.DMA((2,)),
        ],
        wide_conv, (low, mid, flags, place),
    )
    (output,) = call(
        output_kernel, "output", count // large, (large, large, None, None),
        [((count, model), BF16, large)],
        [], wide_up, (inputs, top, down_full, after(wide, conv_sent)),
    )
    conv_grad = add_up(after(conv_kept, output), [swap(conv_sent, *axes[2], 1)])
    conv_stage = scatter_stage(conv_grad, axes[0])
    up_low, mid_sums = call(
        mid_grad_kernel, "mid_grad", steps + 1, (None, None, "past", None, "now", "past"),
        [((count, inner), BF16, "past"), ((24, inner), F32, None)],
        [
            padded,
            pltpu.VMEM((block, KERNEL * inner), BF16),
            pltpu.VMEM((block, inner), F32),
            pltpu.VMEM((block, inner), F32),
        ],
        wide_conv, (low, conv_flat, up_out, after(narrow, conv_grad), flags, flags),
    )
    up_kept, up_sent = call(
        up_weight_kernel, "up_weight", 4, ("early half", "late half", None, None, "smem"),
        [((dp, columns, 2, share, inner), BF16, "any")] * 2,
        [
            pltpu.VMEM((model // 2, inner), F32),
            pltpu.VMEM((2, dp, columns, 2, share, inner), BF16),
            pltpu.SemaphoreType.DMA((2,)),
        ],
        1, (act_one, cotangent, up_low, top, place),
    )
    conv_arrived = after(tuple(conv_stage[1]), up_kept)
    up_grad = add_up(up_kept, [swap(after(up_sent, *conv_arrived), *axes[2], 1)])
    up_stage = scatter_stage(up_grad, axes[0])
    conv_grad = add_up(conv_stage[0], conv_arrived)
    conv_stage = scatter_stage(conv_grad, axes[1])
    input_grad, small_kept, small_sent = call(
        input_grad_kernel, "input_grad", steps + 1,
        ("now", None, "past", "past", None, None, None, None, "smem"),
        [((count, model), F32, "past")] + [((dp, columns, 16, 128), F32, "any")] * 2,
        [
            pltpu.VMEM((block, model), F32),
            pltpu.VMEM((block, model), F32),
            pltpu.VMEM((16, model), F32),
            pltpu.VMEM((8, model), F32),
            pltpu.VMEM((8, inner), F32),
            pltpu.VMEM((2, dp, columns, 16, 128), F32),
            pltpu.SemaphoreType.DMA((2,)),
        ],
        wide_up,
        (up_low, up_full, inputs, cotangent, wide, top_sums, mid_sums, cot_sums, after(place, conv_grad, up_grad)),
    )
    up_arrived, conv_arrived = after((tuple(up_stage[1]), tuple(conv_stage[1])), small_kept)
    small = small_kept + swap(after(small_sent, *up_arrived, *conv_arrived), *axes[2], 1)
    up_stage = scatter_stage(add_up(up_stage[0], up_arrived), axes[1])
    small_own = exact_stage(exact_stage(small, axes[0]), axes[1])
    conv_own = add_up(conv_stage[0], conv_arrived)[0:conv_share]
    up_own, down_own = add_up(*up_stage)
    wide_row, narrow_row = up_weight.shape[0], conv_weight.shape[1]
    sums = [small_own[at, :wide_row] for at in range(2)]
    sums += [small_own[8 + at, :narrow_row] for at in range(6)]
    sums.append(small_own[2, :wide_row])
    return (output, input_grad, up_own, conv_own.reshape(conv_weight.shape), down_own.T) + tuple(sums)


def solution(mesh):
    rows, columns = mesh.shape["dp"], mesh.shape["fsdp"] // 2
    split = Mesh(mesh.devices.reshape(rows, columns, 2), ALL)
    axes = (("dp", rows), ("chip", columns), ("core", 2))
    by_row = P(ALL)
    by_second = P(None, ALL)
    in_specs = [by_row] * 16
    in_specs[10] = in_specs[14] = by_second
    out_specs = [by_row] * 14
    out_specs[3] = out_specs[4] = by_second
    return jax.shard_map(
        functools.partial(body, axes),
        mesh=split,
        in_specs=tuple(in_specs),
        out_specs=tuple(out_specs),
        check_vma=False,
    )
```
